32 devices in a mesh: grp: 2 (over x), ep: 16 (over z, y, core).
Axes of the slice: x: 2, y: 2, z: 4, core: 2. Of those that a mesh axis runs over, the one named last changes fastest.
Arguments:
- hidden_in: bfloat16 [2048, 4096], P(('grp', 'ep')), parts along dimension 0, may hold values from -3 to 3
- queries: bfloat16 [2048, 4096], P(('grp', 'ep')), parts along dimension 0, may hold values from -6 to 6
- token_keys: bfloat16 [2048, 256], P(('grp', 'ep')), parts along dimension 0, may hold values from -6 to 6
- token_values: bfloat16 [2048, 256], P(('grp', 'ep')), parts along dimension 0, may hold values from -15 to 15
- stored_keys: bfloat16 [32768, 256], P(('grp', 'ep')), parts along dimension 0, may hold values from -6 to 6
- stored_values: bfloat16 [32768, 256], P(('grp', 'ep')), parts along dimension 0, may hold values from -15 to 15
- cache_len: int32 [32], P(('grp', 'ep')), parts along dimension 0, may hold values from 1 to 1024, 8192 in all
- query_gain: float32 [128], replicated, may hold values from 0.5 to 2.5
- k_gain: float32 [128], replicated, may hold values from 0.25 to 1.75
- norm_gain: float32 [4096], replicated, may hold values from 0.25 to 1.75
- expert_ids: int32 [2048, 2], P(('grp', 'ep')), parts along dimension 0, may hold values from 0 to 7, as said below
- gate_weights: float32 [2048, 2], P(('grp', 'ep')), parts along dimension 0, may hold values from 0.05 to 0.6
- w_gate: bfloat16 [4096, 6144], P(None, 'ep'), may hold values from -0.09375 to 0.09375
- w_up: bfloat16 [4096, 6144], P(None, 'ep'), may hold values from -0.09375 to 0.09375
- w_down: bfloat16 [6144, 4096], P('ep'), may hold values from -0.21875 to 0.21875
Outputs:
- layer_out: bfloat16 [2048, 4096], P(('grp', 'ep')), parts along dimension 0
The draws below stay inside these ranges and needn't reach their ends.
There are 2 independent parts, one for each index of `grp`. The reference program is written for one: setup_inputs(seed, part) draws one part's arguments, and reference() takes and returns one part's arrays. A program takes and returns all parts, laid end to end along the dimension named above; an argument that names none is the same for every part. Nothing has to cross between parts.
Inputs may be any that keep to these rules, and one draw needn't show every extreme that they name: `expert_ids`: each row names 2 different experts. In each aligned block of 32 rows no expert is named by more than 16 rows, and one expert, the same in every block, is named by exactly 16 rows in every block.
All inputs are finite; a program needn't handle non-finite values. No bound on the sum of `cache_len` on one device may be relied on, other than what follows from the above.
Results may differ from the reference program's by a relative error of at most 0.0095.
Values may be sent and summed in bfloat16 or wider, within the bound.
No kernel may reach another device: no remote copies, remote signals or barrier semaphores. Data moves between devices by JAX's collectives and lax.ppermute only.
A program may use at most 128 MiB of HBM per device.

```python
import math
import jax
import jax.numpy as jnp
import numpy as np
from jax import lax

D = 4096
HEAD_SIZE = 128
QUERY_HEADS = 32
KEY_HEADS = 2
FF = 768
TOKENS_PER_SEQ = 64
CACHE_SLOTS = 1024
EXPERTS = 8
TOP = 2
HALF = 32
MOST = 16
TOKEN_TOTAL = 1024
CACHE_TOTAL = 16384
N_EP = 16


def draw_expert_ids(key, part):
    key = jax.random.fold_in(key, 11)
    hot_expert = jax.random.randint(jax.random.fold_in(key, 1), (), 0, EXPERTS).astype(jnp.int32)
    blocks = TOKEN_TOTAL // HALF
    block_keys = jax.random.split(jax.random.fold_in(key, 2), blocks)
    free_count = HALF * TOP - MOST

    def one_block(block_key):
        key_a, key_b = jax.random.split(block_key)
        row_perm = jax.random.permutation(key_a, HALF).astype(jnp.int32)
        hot_row = jnp.argsort(row_perm) < MOST
        others = jax.random.permutation(key_b, EXPERTS - 1).astype(jnp.int32)
        others = others + (others >= hot_expert).astype(jnp.int32)
        ranks = jnp.arange(EXPERTS - 1, dtype=jnp.int32)
        run_sizes = MOST - ranks % MOST
        run_ends = jnp.cumsum(run_sizes)
        positions = jnp.arange(free_count, dtype=jnp.int32)
        run_index = jnp.sum((run_ends[None, :] <= positions[:, None]).astype(jnp.int32), axis=1)
        expert_seq = others[run_index]
        free_cell = jnp.ones((TOP, HALF), bool).at[0].set(jnp.logical_not(hot_row)).reshape(-1)
        free_index = jnp.cumsum(free_cell.astype(jnp.int32)) - 1
        id_grid = jnp.where(free_cell, expert_seq[jnp.clip(free_index, 0, free_count - 1)], hot_expert)
        return id_grid.reshape(TOP, HALF).T
    return jax.vmap(one_block)(block_keys).reshape(TOKEN_TOTAL, TOP).astype(jnp.int32)


def level_of(own_key, extent, shards, least, largest):
    def one(position, shards_of):
        heights = jax.random.uniform(jax.random.fold_in(jax.random.fold_in(own_key, 6), position), (shards_of,), jnp.float32, least / len(shards), largest / len(shards))
        return jnp.repeat(jnp.exp(heights), extent[position] // shards_of).reshape((-1,) + (1,) * (len(extent) - position - 1))

    loudness = one(*shards[0])
    for cut in shards[1:]:
        loudness = loudness * one(*cut)
    return loudness


def length_profile(amount, total, reach, slope):
    weights = [(1 << 20) // math.isqrt(rank ** slope) + 1 for rank in range(2, amount + 1)]
    rest, given = total - reach - (amount - 1), [1] * (amount - 1)
    while rest > 0:
        movable = [i for i in range(amount - 1) if given[i] < reach]
        whole, left = sum([weights[i] for i in movable]), rest
        for i in movable:
            extra = min(reach - given[i], max(1, left * weights[i] // whole), rest)
            given[i] = given[i] + extra
            rest = rest - extra
    return np.array([reach] + given)


def uneven(key, number_of, total, limit, slope):
    if number_of == 2:
        one = jax.random.randint(key, (), max(1, total - limit), min(limit, total - 1) + 1)
        return jnp.stack([one, total - one])
    sizes = jnp.asarray(length_profile(number_of, total, limit, slope), jnp.int32)
    pairs = (number_of - 1) // 2
    giver, taker = sizes[1:1 + 2 * pairs:2], sizes[2:2 + 2 * pairs:2]
    slack = jnp.minimum(giver - 1, limit - taker)
    shifted = jax.random.randint(jax.random.fold_in(key, 1), (pairs,), 0, 1 << 20) % (slack + 1)
    sizes = sizes.at[1:1 + 2 * pairs:2].set(giver - shifted).at[2:2 + 2 * pairs:2].set(taker + shifted)
    return sizes[jax.random.permutation(jax.random.fold_in(key, 2), number_of)]


def gaussian(rng, dims, deviation, limit, cuts=(), kind=jnp.bfloat16):
    level = level_of(rng, dims, cuts, -0.22, 0.18) if cuts else 1.0
    array = jax.random.normal(rng, dims, jnp.float32) * deviation * level
    return jnp.minimum(jnp.maximum(array, -limit), limit).astype(kind)


def setup_inputs(seed: int = 0, part: int = 0) -> dict:
    keys = jax.random.split(jax.random.key(seed), 16)
    part_keys = jax.random.split(jax.random.fold_in(keys[15], part), 16)
    hidden_in = gaussian(part_keys[0], (TOKEN_TOTAL, D), 0.5, 3.0, ((0, 16),))
    queries = gaussian(part_keys[1], (TOKEN_TOTAL, D), 1.0, 6.0, ((0, 16),))
    token_keys = gaussian(part_keys[2], (TOKEN_TOTAL, KEY_HEADS * HEAD_SIZE), 1.0, 6.0, ((0, 16),))
    token_values = gaussian(part_keys[3], (TOKEN_TOTAL, KEY_HEADS * HEAD_SIZE), 3.0, 15.0, ((0, 16),))
    stored_keys = gaussian(part_keys[4], (CACHE_TOTAL, KEY_HEADS * HEAD_SIZE), 1.0, 6.0, ((0, 16),))
    stored_values = gaussian(part_keys[5], (CACHE_TOTAL, KEY_HEADS * HEAD_SIZE), 3.0, 15.0, ((0, 16),))
    cache_len = uneven(part_keys[6], N_EP, N_EP * CACHE_SLOTS // 2, CACHE_SLOTS, 2).astype(jnp.int32)
    query_gain = jnp.clip(jnp.exp(jax.random.uniform(keys[7], (HEAD_SIZE,), jnp.float32, math.log(0.5), math.log(2.5))), 0.5, 2.5)
    k_gain = jnp.clip(1.0 + 0.15 * jax.random.normal(keys[8], (HEAD_SIZE,), jnp.float32), 0.25, 1.75)
    norm_gain = jnp.clip(1.0 + 0.15 * jax.random.normal(keys[9], (D,), jnp.float32), 0.25, 1.75)
    expert_ids = draw_expert_ids(jax.random.fold_in(jax.random.fold_in(keys[15], part), 71), part)
    gate_weights = jnp.clip(jnp.exp(math.log(0.6) - 2.4849067 * jax.random.uniform(part_keys[11], (TOKEN_TOTAL, TOP), jnp.float32) ** level_of(part_keys[11], (TOKEN_TOTAL, TOP), ((0, 16),), -0.2, 0.2)), 0.05, 0.6)
    w_gate = gaussian(keys[12], (D, EXPERTS * FF), D ** -0.5, 0.09375, ((1, 16),))
    w_up = gaussian(keys[13], (D, EXPERTS * FF), D ** -0.5, 0.09375, ((1, 16),))
    w_down = gaussian(keys[14], (EXPERTS * FF, D), FF ** -0.5, 0.21875, ((0, 16),))
    return {"hidden_in": hidden_in, "queries": queries, "token_keys": token_keys, "token_values": token_values, "stored_keys": stored_keys, "stored_values": stored_values, "cache_len": cache_len, "query_gain": query_gain, "k_gain": k_gain, "norm_gain": norm_gain, "expert_ids": expert_ids, "gate_weights": gate_weights, "w_gate": w_gate, "w_up": w_up, "w_down": w_down}


EPS = 1e-06

def normalized_rows(values_in, gain_vec):
    return values_in * lax.rsqrt(lax.optimization_barrier(jnp.mean(values_in * values_in, axis=-1, keepdims=True)) + EPS) * gain_vec

def attend_one(inputs, query_gain, k_gain):
    query_slice, fresh_keys, fresh_values, prior_keys, prior_values, length = inputs
    query_groups = QUERY_HEADS // KEY_HEADS
    query_normalized = normalized_rows(query_slice.reshape(TOKENS_PER_SEQ, KEY_HEADS, query_groups, HEAD_SIZE).astype(jnp.float32), query_gain).astype(jnp.bfloat16)
    joined_keys = jnp.concatenate([prior_keys, fresh_keys], axis=0).reshape(CACHE_SLOTS + TOKENS_PER_SEQ, KEY_HEADS, HEAD_SIZE)
    key_normed = normalized_rows(joined_keys.astype(jnp.float32), k_gain).astype(jnp.bfloat16)
    joined_values = jnp.concatenate([prior_values, fresh_values], axis=0).reshape(CACHE_SLOTS + TOKENS_PER_SEQ, KEY_HEADS, HEAD_SIZE)
    scores = jnp.einsum('tkgd,skd->ktgs', query_normalized.astype(jnp.float32), key_normed.astype(jnp.float32)) / math.sqrt(HEAD_SIZE)
    key_spots = jnp.arange(CACHE_SLOTS + TOKENS_PER_SEQ, dtype=jnp.int32)
    query_rows = jnp.arange(TOKENS_PER_SEQ, dtype=jnp.int32)
    live_key = jnp.where(key_spots[None, :] < CACHE_SLOTS, key_spots[None, :] < length, key_spots[None, :] - CACHE_SLOTS <= query_rows[:, None])
    raised = jnp.where(live_key[None, :, None, :], jnp.exp(scores), 0.0)
    probs = (raised / lax.optimization_barrier(jnp.sum(raised, axis=-1, keepdims=True))).astype(jnp.bfloat16)
    attended = jnp.einsum('ktgs,skd->tkgd', probs.astype(jnp.float32), joined_values.astype(jnp.float32)).astype(jnp.bfloat16)
    return attended.reshape(TOKENS_PER_SEQ, QUERY_HEADS * HEAD_SIZE)

def reference(hidden_in, queries, token_keys, token_values, stored_keys, stored_values, cache_len, query_gain, k_gain, norm_gain, expert_ids, gate_weights, w_gate, w_up, w_down):
    key_value_width = KEY_HEADS * HEAD_SIZE
    per_sequence = (queries.reshape(N_EP, TOKENS_PER_SEQ, D), token_keys.reshape(N_EP, TOKENS_PER_SEQ, key_value_width), token_values.reshape(N_EP, TOKENS_PER_SEQ, key_value_width), stored_keys.reshape(N_EP, CACHE_SLOTS, key_value_width), stored_values.reshape(N_EP, CACHE_SLOTS, key_value_width), cache_len)
    attended_all = lax.map(lambda inputs: attend_one(inputs, query_gain, k_gain), per_sequence).reshape(TOKEN_TOTAL, D)
    residual = hidden_in.astype(jnp.float32) + attended_all.astype(jnp.float32)
    normed_rows = normalized_rows(residual, norm_gain).astype(jnp.bfloat16)
    flat_ids = expert_ids.reshape(-1)
    flat_gates = gate_weights.reshape(-1)
    per_expert = jax.ops.segment_sum(jnp.ones_like(flat_ids), flat_ids, num_segments=EXPERTS)
    starts = jnp.cumsum(per_expert) - per_expert
    capacity = 2 * N_EP * MOST
    sorted_choice = jnp.concatenate([jnp.argsort(flat_ids, stable=True).astype(jnp.int32), jnp.zeros((capacity,), jnp.int32)])
    half_units = FF // 2

    def one_expert(combined, expert):
        chosen = lax.dynamic_slice_in_dim(sorted_choice, starts[expert].astype(jnp.int32), capacity)
        live_row = jnp.arange(capacity, dtype=jnp.int32) < per_expert[expert]
        token_rows = chosen // TOP
        inputs_here = normed_rows[token_rows]
        gate_cols = lax.dynamic_slice_in_dim(w_gate, expert * FF, FF, 1)
        up_cols = lax.dynamic_slice_in_dim(w_up, expert * FF, FF, 1)
        down_rows = lax.dynamic_slice_in_dim(w_down, expert * FF, FF, 0)
        gate_pre = jnp.dot(inputs_here, gate_cols, preferred_element_type=jnp.float32)
        up_pre = jnp.dot(inputs_here, up_cols, preferred_element_type=jnp.float32)
        inner = (jax.nn.silu(gate_pre) * up_pre).astype(jnp.bfloat16)
        half_a = jnp.dot(inner[:, :half_units], down_rows[:half_units], preferred_element_type=jnp.float32).astype(jnp.bfloat16)
        half_b = jnp.dot(inner[:, half_units:], down_rows[half_units:], preferred_element_type=jnp.float32).astype(jnp.bfloat16)
        expert_out = (half_a.astype(jnp.float32) + half_b.astype(jnp.float32)).astype(jnp.bfloat16)
        weight = jnp.where(live_row, flat_gates[chosen], 0.0)
        combined = combined.at[token_rows].add(weight[:, None] * expert_out.astype(jnp.float32))
        return (combined, None)
    combined, _ = lax.scan(one_expert, jnp.zeros((TOKEN_TOTAL, D), jnp.float32), jnp.arange(EXPERTS, dtype=jnp.int32))
    return (residual + combined).astype(jnp.bfloat16)
```

```python
import math

import jax
import jax.numpy as jnp
from jax import lax
from jax.experimental import pallas as pl
from jax.experimental.pallas import tpu as pltpu
from jax.sharding import PartitionSpec as P

EPS = 1e-06
MIB = 1 << 20
VMEM = pltpu.VMEM
SMEM = pltpu.SMEM


def exchange(value, distance):
    return lax.ppermute(value, "ep", [(i, i ^ distance) for i in range(lax.axis_size("ep"))])


def whole(array):
    return pl.BlockSpec(array.shape, lambda: (0,) * array.ndim, memory_space=VMEM)


def params(mib):
    return pltpu.CompilerParams(vmem_limit_bytes=mib * MIB)


def cost(flops, moved):
    return pl.CostEstimate(flops=int(flops), bytes_accessed=int(moved), transcendentals=0)


def slots_of(chip, half, cap):
    lane = lax.broadcasted_iota(jnp.int32, (1, half * cap), 1)
    apart = lane // cap
    position = chip & (half - 1)
    expert = (chip - position) + (apart ^ position)
    return expert.astype(jnp.float32), (lane - apart * cap).astype(jnp.float32)


def slot_hits(info, expert, slot):
    rows, width = info.shape
    top = width // 2
    named = info[:, 0:1] == expert
    for k in range(1, top):
        named = jnp.logical_or(named, info[:, k : k + 1] == expert)
    row = lax.broadcasted_iota(jnp.int32, (rows, rows), 0)
    col = lax.broadcasted_iota(jnp.int32, (rows, rows), 1)
    earlier = jnp.where(col < row, 1.0, 0.0).astype(jnp.bfloat16)
    ones = jnp.where(named, 1.0, 0.0)
    rank = jnp.dot(earlier, ones.astype(jnp.bfloat16), preferred_element_type=jnp.float32)
    return jnp.where(rank == slot, ones, 0.0)


def spread_rows(chip, info, rows_bf16, out_refs, cap):
    half = len(out_refs)
    expert, slot = slots_of(chip, half, cap)
    hits = slot_hits(info, expert, slot).astype(jnp.bfloat16)
    for d in range(half):
        out_refs[d][...] = lax.dot_general(
            hits[:, d * cap : (d + 1) * cap],
            rows_bf16,
            (((0,), (0,)), ((), ())),
            preferred_element_type=jnp.float32,
        ).astype(jnp.bfloat16)


def weighted_rows(chip, info, in_refs, joined, cap):
    half = len(in_refs)
    top = info.shape[1] // 2
    expert, slot = slots_of(chip, half, cap)
    hits = slot_hits(info, expert, slot)
    weight = jnp.zeros_like(hits)
    for k in range(top):
        weight = weight + jnp.where(info[:, k : k + 1] == expert, info[:, top + k : top + k + 1], 0.0)
    weight = weight * hits
    high = weight.astype(jnp.bfloat16)
    low = (weight - high.astype(jnp.float32)).astype(jnp.bfloat16)
    for d in range(half):
        joined[d * cap : (d + 1) * cap, :] = in_refs[d][...]
    values = joined[...]
    return jnp.dot(high, values, preferred_element_type=jnp.float32) + jnp.dot(
        low, values, preferred_element_type=jnp.float32
    )


def unit_rows(values, gain):
    return values * lax.rsqrt(jnp.mean(values * values, axis=-1, keepdims=True) + EPS) * gain


def attend_kernel(cap, first_token, *refs):
    (meta, q_ref, hid_ref, sk_ref, tk_ref, sv_ref, tv_ref, qg_ref, kg_ref, ng_ref, info_ref) = refs[:11]
    (resid_ref, normed_ref, *out_refs) = refs[11:-3]
    kn_ref, vx_ref, qs_ref = refs[-3:]
    rows, width = resid_ref.shape
    mine = slice(first_token, first_token + rows)
    cache_rows = sk_ref.shape[0]
    token_rows = tk_ref.shape[0]
    head = qg_ref.shape[1]
    heads_kv = sk_ref.shape[1] // head
    heads = width // head
    group = heads // heads_kv
    length = meta[0]
    chip = meta[1]
    keys = cache_rows + token_rows
    q_gain = qg_ref[...] * (math.log2(math.e) / math.sqrt(head))
    k_gain = kg_ref[...]
    live = lax.broadcasted_iota(jnp.int32, (cache_rows, head), 0) < length
    live_ones = jnp.where(live, 1.0, 0.0).astype(jnp.bfloat16)
    for g in range(heads_kv):
        cols = slice(g * head, (g + 1) * head)
        kn_ref[g, :cache_rows, :] = unit_rows(sk_ref[:, cols].astype(jnp.float32), k_gain).astype(jnp.bfloat16)
        kn_ref[g, cache_rows:, :] = unit_rows(tk_ref[:, cols].astype(jnp.float32), k_gain).astype(jnp.bfloat16)
        vx_ref[g, :cache_rows, :head] = jnp.where(live, sv_ref[:, cols].astype(jnp.float32), 0.0).astype(jnp.bfloat16)
        vx_ref[g, :cache_rows, head:] = live_ones
        vx_ref[g, cache_rows:, :head] = tv_ref[:, cols]
        vx_ref[g, cache_rows:, head:] = jnp.ones((token_rows, head), jnp.bfloat16)
    for h in range(heads):
        x = q_ref[mine, h * head : (h + 1) * head].astype(jnp.float32)
        qs_ref[h * rows : (h + 1) * rows, :] = unit_rows(x, q_gain).astype(jnp.bfloat16)
    per = max(1, min(group, 256 // rows))
    block = per * rows
    own = lax.broadcasted_iota(jnp.int32, (block, token_rows), 0) % rows + first_token
    spot = lax.broadcasted_iota(jnp.int32, (block, token_rows), 1)
    causal = spot <= own
    square = jnp.zeros((rows, head), jnp.float32)
    for b in range(heads // per):
        g = b * per // group
        q_block = qs_ref[b * block : (b + 1) * block, :]
        scores = lax.dot_general(
            q_block, kn_ref[g, :cache_rows, :], (((1,), (1,)), ((), ())), preferred_element_type=jnp.float32
        )
        raised = jnp.exp2(scores).astype(jnp.bfloat16)
        scores_new = lax.dot_general(
            q_block, kn_ref[g, cache_rows:, :], (((1,), (1,)), ((), ())), preferred_element_type=jnp.float32
        )
        raised_new = jnp.where(causal, jnp.exp2(scores_new), 0.0).astype(jnp.bfloat16)
        summed = jnp.dot(raised, vx_ref[g, :cache_rows, :], preferred_element_type=jnp.float32) + jnp.dot(
            raised_new, vx_ref[g, cache_rows:, :], preferred_element_type=jnp.float32
        )
        attended = (summed[:, :head] / summed[:, head:]).astype(jnp.bfloat16).astype(jnp.float32)
        for i in range(per):
            cols = slice((b * per + i) * head, (b * per + i + 1) * head)
            resid = hid_ref[mine, cols].astype(jnp.float32) + attended[i * rows : (i + 1) * rows, :]
            resid_ref[:, cols] = resid
            square = square + resid * resid
    scale = lax.rsqrt(jnp.sum(square, axis=-1, keepdims=True) / width + EPS)
    normed = (resid_ref[...] * scale * ng_ref[...]).astype(jnp.bfloat16)
    normed_ref[...] = normed
    spread_rows(chip, info_ref[mine, :], normed, out_refs, cap)


def attend(meta, arrays, gains, info, chunk, chunks, half, cap):
    hidden_in, queries, token_keys, token_values, stored_keys, stored_values = arrays
    query_gain, k_gain, norm_gain = gains
    rows, width = hidden_in.shape[0] // chunks, hidden_in.shape[1]
    cache_rows, kv_width = stored_keys.shape
    token_rows = token_keys.shape[0]
    head = query_gain.shape[1]
    heads_kv = kv_width // head
    keys = cache_rows + token_rows
    out_shape = [
        jax.ShapeDtypeStruct((rows, width), jnp.float32),
        jax.ShapeDtypeStruct((rows, width), jnp.bfloat16),
    ] + [jax.ShapeDtypeStruct((cap, width), jnp.bfloat16)] * half

    def body(*refs):
        attend_kernel(cap, chunk * rows, *refs)

    results = pl.pallas_call(
        body,
        out_shape=out_shape,
        in_specs=[
            pl.BlockSpec(memory_space=SMEM),
            whole(queries),
            whole(hidden_in),
            whole(stored_keys),
            whole(token_keys),
            whole(stored_values),
            whole(token_values),
            whole(query_gain),
            whole(k_gain),
            whole(norm_gain),
            whole(info),
        ],
        out_specs=[pl.BlockSpec(o.shape, lambda: (0, 0), memory_space=VMEM) for o in out_shape],
        scratch_shapes=[
            VMEM((heads_kv, keys, head), jnp.bfloat16),
            VMEM((heads_kv, keys, 2 * head), jnp.bfloat16),
            VMEM((rows * width // head, head), jnp.bfloat16),
        ],
        compiler_params=params(32),
        cost_estimate=cost(4 * rows * width * keys, 6 * MIB),
        name="attend",
    )(meta, queries, hidden_in, stored_keys, token_keys, stored_values, token_values, query_gain, k_gain, norm_gain, info)
    return results[0], results[1], list(results[2:])


def relay(meta, rows_in, info, chunk, half, cap):
    rows, width = rows_in.shape
    out = jax.ShapeDtypeStruct((cap, width), jnp.bfloat16)

    def body(meta_ref, rows_ref, info_ref, *out_refs):
        spread_rows(meta_ref[1], info_ref[chunk * rows : (chunk + 1) * rows, :], rows_ref[...], out_refs, cap)

    return list(
        pl.pallas_call(
            body,
            out_shape=[out] * half,
            in_specs=[pl.BlockSpec(memory_space=SMEM), whole(rows_in), whole(info)],
            out_specs=[whole(out)] * half,
            compiler_params=params(32),
            cost_estimate=cost(2 * half * cap * rows * width, MIB),
            name="relay",
        )(meta, rows_in, info)
    )


def expert(own, other, w_gate, w_up, w_down):
    cap, width = own[0].shape
    count = len(own)
    hidden = w_gate.shape[1]
    total = 2 * count * cap
    block = min(total, 256)
    steps = 4
    k_part = width // steps
    out = jax.ShapeDtypeStruct((count * cap, width), jnp.bfloat16)

    def body(*refs):
        ins = refs[: 2 * count]
        wg_hbm, wu_hbm, wd_hbm = refs[2 * count : 2 * count + 3]
        out_own, out_other = refs[2 * count + 3 : 2 * count + 5]
        x_ref, y_ref, wgu, wd, sems = refs[2 * count + 5 :]
        up_copies, down_copies = [], []
        for s in range(steps):
            part = pl.ds(s * k_part, k_part)
            up_copies.append(
                (
                    pltpu.make_async_copy(wg_hbm.at[part, :], wgu.at[part, pl.ds(0, hidden)], sems.at[0, s]),
                    pltpu.make_async_copy(wu_hbm.at[part, :], wgu.at[part, pl.ds(hidden, hidden)], sems.at[1, s]),
                )
            )
            down_copies.append(pltpu.make_async_copy(wd_hbm.at[:, part], wd.at[:, part], sems.at[2, s]))
        for pair in up_copies:
            for copy in pair:
                copy.start()
        for copy in down_copies:
            copy.start()
        for i in range(2 * count):
            x_ref[i * cap : (i + 1) * cap, :] = ins[i][...]

        def rows_of(r, waiting):
            span = pl.ds(r * block, block) if isinstance(r, int) else pl.ds(pl.multiple_of(r * block, block), block)
            pre = jnp.zeros((block, 2 * hidden), jnp.float32)
            for s in range(steps):
                if waiting:
                    for copy in up_copies[s]:
                        copy.wait()
                pre = pre + jnp.dot(
                    x_ref[span, s * k_part : (s + 1) * k_part],
                    wgu[s * k_part : (s + 1) * k_part, :],
                    preferred_element_type=jnp.float32,
                )
            gate = pre[:, :hidden]
            inner = (gate / (1.0 + jnp.exp(-gate)) * pre[:, hidden:]).astype(jnp.bfloat16)
            for s in range(steps):
                if waiting:
                    down_copies[s].wait()
                y_ref[span, s * k_part : (s + 1) * k_part] = jnp.dot(
                    inner, wd[:, s * k_part : (s + 1) * k_part], preferred_element_type=jnp.float32
                ).astype(jnp.bfloat16)

        rows_of(0, True)
        if total > block:

            @pl.loop(1, total // block)
            def _(r):
                rows_of(r, False)

        out_own[...] = y_ref[: count * cap, :]
        out_other[...] = y_ref[count * cap :, :]

    return pl.pallas_call(
        body,
        out_shape=[out, out],
        in_specs=[whole(own[0])] * (2 * count) + [pl.BlockSpec(memory_space=pl.ANY)] * 3,
        out_specs=[whole(out)] * 2,
        scratch_shapes=[
            VMEM((total, width), jnp.bfloat16),
            VMEM((total, width), jnp.bfloat16),
            VMEM((width, 2 * hidden), jnp.bfloat16),
            VMEM((hidden, width), jnp.bfloat16),
            pltpu.SemaphoreType.DMA((3, steps)),
        ],
        compiler_params=params(52),
        cost_estimate=cost(6 * total * width * hidden, 6 * width * hidden),
        name="expert",
    )(*own, *other, w_gate, w_up, w_down)


def add_halves(mine, theirs, cap):
    rows, width = mine.shape
    count = rows // cap
    out = jax.ShapeDtypeStruct((cap, width), jnp.bfloat16)

    def body(a_ref, b_ref, *out_refs):
        for i in range(count):
            span = slice(i * cap, (i + 1) * cap)
            out_refs[i][...] = (a_ref[span, :].astype(jnp.float32) + b_ref[span, :].astype(jnp.float32)).astype(
                jnp.bfloat16
            )

    return list(
        pl.pallas_call(
            body,
            out_shape=[out] * count,
            in_specs=[whole(mine)] * 2,
            out_specs=[whole(out)] * count,
            compiler_params=params(32),
            cost_estimate=cost(rows * width, 6 * rows * width),
            name="add_halves",
        )(mine, theirs)
    )


def relay_back(meta, returned, info, chunk, rows, cap):
    half = len(returned)
    width = returned[0].shape[1]
    out = jax.ShapeDtypeStruct((rows, width), jnp.bfloat16)

    def body(meta_ref, info_ref, *refs):
        in_refs, out_ref, joined = refs[:half], refs[half], refs[half + 1]
        out_ref[...] = weighted_rows(meta_ref[1], info_ref[chunk * rows : (chunk + 1) * rows, :], in_refs, joined, cap).astype(jnp.bfloat16)

    return pl.pallas_call(
        body,
        out_shape=out,
        in_specs=[pl.BlockSpec(memory_space=SMEM), whole(info)]
        + [whole(returned[0])] * half,
        out_specs=whole(out),
        scratch_shapes=[VMEM((half * cap, width), jnp.bfloat16)],
        compiler_params=params(32),
        cost_estimate=cost(4 * half * cap * rows * width, MIB),
        name="relay_back",
    )(meta, info, *returned)


def finish(meta, resid, returned, far, info, chunk, chunks, cap, previous):
    half = len(returned)
    rows, width = resid.shape
    out = jax.ShapeDtypeStruct((rows * chunks, width), jnp.bfloat16)
    extra = [] if previous is None else [previous]

    def body(*refs):
        refs = refs[len(extra) :]
        meta_ref, info_ref, resid_ref, far_ref = refs[:4]
        in_refs, out_hbm, joined, out_ref, sem = refs[4 : 4 + half], *refs[4 + half :]
        near = weighted_rows(meta_ref[1], info_ref[chunk * rows : (chunk + 1) * rows, :], in_refs, joined, cap)
        out_ref[...] = (resid_ref[...] + (near + far_ref[...].astype(jnp.float32))).astype(jnp.bfloat16)
        copy = pltpu.make_async_copy(out_ref, out_hbm.at[pl.ds(chunk * rows, rows), :], sem)
        copy.start()
        copy.wait()

    return pl.pallas_call(
        body,
        out_shape=out,
        in_specs=[pl.BlockSpec(memory_space=pl.ANY)] * len(extra)
        + [
            pl.BlockSpec(memory_space=SMEM),
            whole(info),
            whole(resid),
            whole(far),
        ]
        + [whole(returned[0])] * half,
        out_specs=pl.BlockSpec(memory_space=pl.ANY),
        scratch_shapes=[
            VMEM((half * cap, width), jnp.bfloat16),
            VMEM((rows, width), jnp.bfloat16),
            pltpu.SemaphoreType.DMA,
        ],
        input_output_aliases={0: 0} if extra else {},
        compiler_params=params(32),
        cost_estimate=cost(4 * half * cap * rows * width, 2 * MIB),
        name="finish",
    )(*extra, meta, info, resid, far, *returned)


def local(
    hidden_in,
    queries,
    token_keys,
    token_values,
    stored_keys,
    stored_values,
    cache_len,
    query_gain,
    k_gain,
    norm_gain,
    expert_ids,
    gate_weights,
    w_gate,
    w_up,
    w_down,
):
    token_rows, top = expert_ids.shape
    ep = lax.axis_size("ep")
    experts = ep // 2
    half = experts // 2
    slots = 2 * token_rows * top // experts
    chunks = 2 if slots >= 32 else 1
    cap = slots // chunks
    rows = token_rows // chunks
    chip = lax.axis_index("ep") // 2
    meta = jnp.stack([cache_len[0], chip.astype(jnp.int32)])
    info = jnp.concatenate([expert_ids.astype(jnp.float32), gate_weights], axis=1)
    far_info = exchange(info, ep // 2)
    arrays = (hidden_in, queries, token_keys, token_values, stored_keys, stored_values)
    gains = (query_gain[None, :], k_gain[None, :], norm_gain[None, :])

    resid, far_rows, near_own = [], [], []
    for c in range(chunks):
        residual, normed, outgoing = attend(meta, arrays, gains, info, c, chunks, half, cap)
        resid.append(residual)
        far_rows.append(exchange(normed, ep // 2))
        near_own.append([outgoing[0]] + [exchange(outgoing[d], 2 * d) for d in range(1, half)])

    def run_experts(own):
        other = [exchange(x, 1) for x in own]
        mine, theirs = expert(own, other, w_gate, w_up, w_down)
        return add_halves(mine, exchange(theirs, 1), cap)

    def give_back(parts):
        return [parts[0]] + [exchange(parts[d], 2 * d) for d in range(1, half)]

    near_out = run_experts([x for own in near_own for x in own])
    near_back = [give_back(near_out[c * half : (c + 1) * half]) for c in range(chunks)]
    far_back = []
    for c in range(chunks):
        outgoing = relay(meta, far_rows[c], far_info, c, half, cap)
        own = [outgoing[0]] + [exchange(outgoing[d], 2 * d) for d in range(1, half)]
        returned = give_back(run_experts(own))
        far_back.append(exchange(relay_back(meta, returned, far_info, c, rows, cap), ep // 2))
    result = None
    for c in range(chunks):
        result = finish(meta, resid[c], near_back[c], far_back[c], info, c, chunks, cap, result)
    return result


def solution(mesh):
    in_specs = (
        P(("grp", "ep"), None),
        P(("grp", "ep"), None),
        P(("grp", "ep"), None),
        P(("grp", "ep"), None),
        P(("grp", "ep"), None),
        P(("grp", "ep"), None),
        P(("grp", "ep")),
        P(),
        P(),
        P(),
        P(("grp", "ep"), None),
        P(("grp", "ep"), None),
        P(None, "ep"),
        P(None, "ep"),
        P("ep", None),
    )
    out_specs = P(("grp", "ep"), None)
    return jax.shard_map(local, mesh=mesh, in_specs=in_specs, out_specs=out_specs, check_vma=False)
```

```python
import math

import jax
import jax.numpy as jnp
from jax import lax
from jax.experimental import pallas as pl
from jax.experimental.pallas import tpu as pltpu
from jax.sharding import PartitionSpec as P

EPS = 1e-06
MIB = 1 << 20
VMEM = pltpu.VMEM
SMEM = pltpu.SMEM


def exchange(value, distance):
    return lax.ppermute(value, "ep", [(i, i ^ distance) for i in range(lax.axis_size("ep"))])


def whole(array):
    return pl.BlockSpec(array.shape, lambda: (0,) * array.ndim, memory_space=VMEM)


def params(mib):
    return pltpu.CompilerParams(vmem_limit_bytes=mib * MIB)


def cost(flops, moved):
    return pl.CostEstimate(flops=int(flops), bytes_accessed=int(moved), transcendentals=0)


def slots_of(half, cap):
    chip = lax.axis_index("ep") // 2
    lane = lax.broadcasted_iota(jnp.int32, (half * cap, 1), 0)
    apart = lane // cap
    position = chip & (half - 1)
    expert = (chip - position) + (apart ^ position)
    return expert.astype(jnp.float32), (lane - apart * cap).astype(jnp.float32)


def slot_hits(info, expert, slot):
    width, rows = info.shape
    named = info[0:1, :] == expert
    for k in range(1, width // 2):
        named = jnp.logical_or(named, info[k : k + 1, :] == expert)
    row = lax.broadcasted_iota(jnp.int32, (rows, rows), 0)
    col = lax.broadcasted_iota(jnp.int32, (rows, rows), 1)
    earlier = jnp.where(row < col, 1.0, 0.0).astype(jnp.bfloat16)
    ones = jnp.where(named, 1.0, 0.0)
    rank = jnp.dot(ones.astype(jnp.bfloat16), earlier, preferred_element_type=jnp.float32)
    return jnp.where(rank == slot, ones, 0.0)


def spread_rows(info, rows_bf16, out_refs, cap):
    half = len(out_refs)
    expert, slot = slots_of(half, cap)
    hits = slot_hits(info, expert, slot).astype(jnp.bfloat16)
    placed = jnp.dot(hits, rows_bf16, preferred_element_type=jnp.float32).astype(jnp.bfloat16)
    for d in range(half):
        out_refs[d][...] = placed[d * cap : (d + 1) * cap, :]


def weighted_rows(info, half, joined, cap):
    top = info.shape[0] // 2
    expert, slot = slots_of(half, cap)
    hits = slot_hits(info, expert, slot)
    weight = jnp.zeros_like(hits)
    for k in range(top):
        weight = weight + jnp.where(info[k : k + 1, :] == expert, info[top + k : top + k + 1, :], 0.0)
    weight = weight * hits
    high = weight.astype(jnp.bfloat16)
    low = (weight - high.astype(jnp.float32)).astype(jnp.bfloat16)
    values = joined[...]
    first = (((0,), (0,)), ((), ()))
    return lax.dot_general(high, values, first, preferred_element_type=jnp.float32) + lax.dot_general(
        low, values, first, preferred_element_type=jnp.float32
    )


def unit_rows(values, gain):
    return values * lax.rsqrt(jnp.mean(values * values, axis=-1, keepdims=True) + EPS) * gain


def attend(cache_len, arrays, before, chunk, chunks, half, cap):
    queries, hidden_in, stored_keys, stored_values, token_keys, token_values = arrays[:6]
    ids, gates = arrays[9:]
    rows, width = hidden_in.shape[0] // chunks, hidden_in.shape[1]
    cache_rows, kv_width = stored_keys.shape
    token_rows = token_keys.shape[0]
    head = arrays[6].shape[0]
    heads_kv = kv_width // head
    heads = width // head
    group = heads // heads_kv
    keys = cache_rows + token_rows
    top = ids.shape[0]
    first, last = chunk == 0, chunk == chunks - 1
    mine = pl.ds(chunk * rows, rows)
    per = max(1, min(group, 256 // rows))
    block = per * rows
    near_rows = cap * chunks if last else cap
    out_shape = [
        jax.ShapeDtypeStruct((rows, width), jnp.float32),
        jax.ShapeDtypeStruct((rows, width), jnp.bfloat16),
    ]
    out_shape += [jax.ShapeDtypeStruct((near_rows, width), jnp.bfloat16)] * half
    if first:
        out_shape.append(jax.ShapeDtypeStruct((2 * top, token_rows), jnp.float32))

    def body(len_ref, *refs):
        hbm, refs = refs[:11], refs[11:]
        carried, refs = refs[: len(before)], refs[len(before) :]
        outs, scratch = refs[: len(out_shape)], refs[len(out_shape) :]
        (q_ref, hid_ref, sk_ref, sv_ref, tk_ref, tv_ref, qg_ref, kg_ref, ng_ref, ids_ref, gates_ref) = scratch[:11]
        kn_ref, vx_ref, qs_ref, info_ref, sems = scratch[11:]
        resid_ref, normed_ref, out_refs = outs[0], outs[1], outs[2 : 2 + half]
        copies = []
        for i in range(11):
            source = hbm[i].at[mine, :] if i < 2 else hbm[i]
            target = scratch[i].at[0] if 6 <= i < 9 else scratch[i]
            copies.append(pltpu.make_async_copy(source, target, sems.at[i]))
        order = (2, 7, 4, 0, 6, 3, 5, 9, 10, 1, 8)
        for i in order:
            copies[i].start()
        length = len_ref[0]
        live = lax.broadcasted_iota(jnp.int32, (cache_rows, head), 0) < length
        live_ones = jnp.where(live, 1.0, 0.0).astype(jnp.bfloat16)
        for i in (2, 7, 4):
            copies[i].wait()
        k_gain = kg_ref[...]
        for g in range(heads_kv):
            cols = slice(g * head, (g + 1) * head)
            kn_ref[g, :cache_rows, :] = unit_rows(sk_ref[:, cols].astype(jnp.float32), k_gain).astype(jnp.bfloat16)
            kn_ref[g, cache_rows:, :] = unit_rows(tk_ref[:, cols].astype(jnp.float32), k_gain).astype(jnp.bfloat16)
        for i in (0, 6):
            copies[i].wait()
        q_gain = qg_ref[...] * (math.log2(math.e) / math.sqrt(head))
        for h in range(heads):
            x = q_ref[:, h * head : (h + 1) * head].astype(jnp.float32)
            qs_ref[h * rows : (h + 1) * rows, :] = unit_rows(x, q_gain).astype(jnp.bfloat16)
        for i in (3, 5):
            copies[i].wait()
        for g in range(heads_kv):
            cols = slice(g * head, (g + 1) * head)
            vx_ref[g, :cache_rows, :head] = jnp.where(live, sv_ref[:, cols].astype(jnp.float32), 0.0).astype(
                jnp.bfloat16
            )
            vx_ref[g, :cache_rows, head:] = live_ones
            vx_ref[g, cache_rows:, :head] = tv_ref[:, cols]
            vx_ref[g, cache_rows:, head:] = jnp.ones((token_rows, head), jnp.bfloat16)
        for i in (9, 10, 1, 8):
            copies[i].wait()
        info_ref[:top, :] = ids_ref[...].astype(jnp.float32)
        info_ref[top:, :] = gates_ref[...]
        if first:
            outs[-1][...] = info_ref[...]
        own = lax.broadcasted_iota(jnp.int32, (block, token_rows), 0) % rows + chunk * rows
        causal = lax.broadcasted_iota(jnp.int32, (block, token_rows), 1) <= own
        square = jnp.zeros((rows, head), jnp.float32)
        last_dims = (((1,), (1,)), ((), ()))
        for b in range(heads // per):
            g = b * per // group
            q_block = qs_ref[b * block : (b + 1) * block, :]
            scores = lax.dot_general(q_block, kn_ref[g, :cache_rows, :], last_dims, preferred_element_type=jnp.float32)
            raised = jnp.exp2(scores).astype(jnp.bfloat16)
            scores_new = lax.dot_general(
                q_block, kn_ref[g, cache_rows:, :], last_dims, preferred_element_type=jnp.float32
            )
            raised_new = jnp.where(causal, jnp.exp2(scores_new), 0.0).astype(jnp.bfloat16)
            summed = jnp.dot(raised, vx_ref[g, :cache_rows, :], preferred_element_type=jnp.float32) + jnp.dot(
                raised_new, vx_ref[g, cache_rows:, :], preferred_element_type=jnp.float32
            )
            attended = (summed[:, :head] / summed[:, head:]).astype(jnp.bfloat16).astype(jnp.float32)
            for i in range(per):
                cols = slice((b * per + i) * head, (b * per + i + 1) * head)
                resid = hid_ref[:, cols].astype(jnp.float32) + attended[i * rows : (i + 1) * rows, :]
                resid_ref[:, cols] = resid
                square = square + resid * resid
        scale = lax.rsqrt(jnp.sum(square, axis=-1, keepdims=True) / width + EPS)
        normed = (resid_ref[...] * scale * ng_ref[...]).astype(jnp.bfloat16)
        normed_ref[...] = normed
        tail = slice(near_rows - cap, near_rows)
        spread_rows(info_ref[:, chunk * rows : (chunk + 1) * rows], normed, [o.at[tail, :] for o in out_refs], cap)
        for i in range(len(before)):
            out_refs[i][: near_rows - cap, :] = carried[i][...]

    results = pl.pallas_call(
        body,
        out_shape=out_shape,
        in_specs=[pl.BlockSpec(memory_space=SMEM)]
        + [pl.BlockSpec(memory_space=pl.ANY)] * 11
        + [whole(b) for b in before],
        out_specs=[whole(o) for o in out_shape],
        scratch_shapes=[
            VMEM((rows, width), jnp.bfloat16),
            VMEM((rows, width), jnp.bfloat16),
            VMEM((cache_rows, kv_width), jnp.bfloat16),
            VMEM((cache_rows, kv_width), jnp.bfloat16),
            VMEM((token_rows, kv_width), jnp.bfloat16),
            VMEM((token_rows, kv_width), jnp.bfloat16),
            VMEM((1, head), jnp.float32),
            VMEM((1, head), jnp.float32),
            VMEM((1, width), jnp.float32),
            VMEM((top, token_rows), jnp.int32),
            VMEM((top, token_rows), jnp.float32),
            VMEM((heads_kv, keys, head), jnp.bfloat16),
            VMEM((heads_kv, keys, 2 * head), jnp.bfloat16),
            VMEM((rows * heads, head), jnp.bfloat16),
            VMEM((2 * top, token_rows), jnp.float32),
            pltpu.SemaphoreType.DMA((11,)),
        ],
        compiler_params=params(24),
        cost_estimate=cost(4 * rows * width * keys, 6 * MIB),
        name="attend",
    )(cache_len, *arrays, *before)
    return results[0], results[1], list(results[2 : 2 + half]), (results[-1] if first else None)


def relay(rows_in, info, chunk, half, cap):
    rows, width = rows_in.shape
    out = jax.ShapeDtypeStruct((cap, width), jnp.bfloat16)

    def body(rows_ref, info_ref, *out_refs):
        spread_rows(info_ref[:, chunk * rows : (chunk + 1) * rows], rows_ref[...], out_refs, cap)

    return list(
        pl.pallas_call(
            body,
            out_shape=[out] * half,
            in_specs=[whole(rows_in), whole(info)],
            out_specs=[whole(out)] * half,
            compiler_params=params(24),
            cost_estimate=cost(2 * half * cap * rows * width, MIB),
            name="relay",
        )(rows_in, info)
    )


def expert(own, weights):
    cap, width = own[0].shape
    count = len(own)
    hidden = weights[0].shape[1]
    total = count * cap
    block = min(total, 128)
    part = 512
    out = jax.ShapeDtypeStruct((cap, width), jnp.bfloat16)

    def body(*refs):
        ins, (wg0, wu0, wd0, wg1, wu1, wd1) = refs[:count], refs[count : count + 6]
        outs, (x_ref, y_ref) = refs[count + 6 : 2 * count + 6], refs[2 * count + 6 :]
        for i in range(count):
            x_ref[i * cap : (i + 1) * cap, :] = ins[i][...]

        def rows_of(span):
            inners = []
            for wg, wu in ((wg0, wu0), (wg1, wu1)):
                pre = jnp.zeros((block, 2 * hidden), jnp.float32)
                for k in range(0, width, part):
                    both = jnp.concatenate([wg[k : k + part, :], wu[k : k + part, :]], axis=1)
                    pre = pre + jnp.dot(x_ref[span, k : k + part], both, preferred_element_type=jnp.float32)
                gate = pre[:, :hidden]
                inners.append((gate / (1.0 + jnp.exp(-gate)) * pre[:, hidden:]).astype(jnp.bfloat16))
            inner = jnp.concatenate(inners, axis=1)
            for k in range(0, width, part):
                down = jnp.concatenate([wd0[:, k : k + part], wd1[:, k : k + part]], axis=0)
                y_ref[span, k : k + part] = jnp.dot(inner, down, preferred_element_type=jnp.float32).astype(
                    jnp.bfloat16
                )

        if total == block:
            rows_of(slice(0, block))
        else:

            @pl.loop(0, total // block)
            def _(r):
                rows_of(pl.ds(pl.multiple_of(r * block, block), block))

        for i in range(count):
            outs[i][...] = y_ref[i * cap : (i + 1) * cap, :]

    return list(
        pl.pallas_call(
            body,
            out_shape=[out] * count,
            in_specs=[whole(own[0])] * count + [whole(w) for w in weights],
            out_specs=[whole(out)] * count,
            scratch_shapes=[VMEM((total, width), jnp.bfloat16)] * 2,
            compiler_params=params(24),
            cost_estimate=cost(12 * total * width * hidden, 12 * width * hidden),
            name="expert",
        )(*own, *weights)
    )


def relay_back(returned, info, chunk, rows, cap):
    half = len(returned)
    width = returned[0].shape[1]
    out = jax.ShapeDtypeStruct((rows, width), jnp.bfloat16)

    def body(info_ref, *refs):
        in_refs, out_ref, joined = refs[:half], refs[half], refs[half + 1]
        for d in range(half):
            joined[d * cap : (d + 1) * cap, :] = in_refs[d][...]
        far = weighted_rows(info_ref[:, chunk * rows : (chunk + 1) * rows], half, joined, cap)
        out_ref[...] = far.astype(jnp.bfloat16)

    return pl.pallas_call(
        body,
        out_shape=out,
        in_specs=[whole(info)] + [whole(returned[0])] * half,
        out_specs=whole(out),
        scratch_shapes=[VMEM((half * cap, width), jnp.bfloat16)],
        compiler_params=params(24),
        cost_estimate=cost(4 * half * cap * rows * width, MIB),
        name="relay_back",
    )(info, *returned)


def finish(resid, returned, far, info, chunk, chunks, cap, previous):
    half = len(returned)
    rows, width = resid.shape
    out = jax.ShapeDtypeStruct((rows * chunks, width), jnp.bfloat16)
    extra = [] if previous is None else [previous]

    def body(*refs):
        info_ref, resid_ref, far_ref = refs[len(extra) : len(extra) + 3]
        refs = refs[len(extra) + 3 :]
        in_refs, out_hbm, joined, out_ref, sem = refs[:half], *refs[half:]
        for d in range(half):
            joined[d * cap : (d + 1) * cap, :] = in_refs[d][chunk * cap : (chunk + 1) * cap, :]
        near = weighted_rows(info_ref[:, chunk * rows : (chunk + 1) * rows], half, joined, cap)
        out_ref[...] = (resid_ref[...] + (near + far_ref[...].astype(jnp.float32))).astype(jnp.bfloat16)
        copy = pltpu.make_async_copy(out_ref, out_hbm.at[pl.ds(chunk * rows, rows), :], sem)
        copy.start()
        copy.wait()

    return pl.pallas_call(
        body,
        out_shape=out,
        in_specs=[pl.BlockSpec(memory_space=pl.ANY)] * len(extra)
        + [whole(info), whole(resid), whole(far)]
        + [whole(returned[0])] * half,
        out_specs=pl.BlockSpec(memory_space=pl.ANY),
        scratch_shapes=[
            VMEM((half * cap, width), jnp.bfloat16),
            VMEM((rows, width), jnp.bfloat16),
            pltpu.SemaphoreType.DMA,
        ],
        input_output_aliases={0: 0} if extra else {},
        compiler_params=params(24),
        cost_estimate=cost(4 * half * cap * rows * width, 2 * MIB),
        name="finish",
    )(*extra, info, resid, far, *returned)


def around(parts):
    return [parts[0]] + [exchange(parts[d], 2 * d) for d in range(1, len(parts))]


def local(
    hidden_in,
    queries,
    token_keys,
    token_values,
    stored_keys,
    stored_values,
    cache_len,
    query_gain,
    k_gain,
    norm_gain,
    expert_ids,
    gate_weights,
    w_gate,
    w_up,
    w_down,
):
    token_rows, top = expert_ids.shape
    ep = lax.axis_size("ep")
    experts = ep // 2
    half = experts // 2
    slots = 2 * token_rows * top // experts
    chunks = 2 if slots >= 32 else 1
    cap = slots // chunks
    rows = token_rows // chunks
    arrays = (
        queries,
        hidden_in,
        stored_keys,
        stored_values,
        token_keys,
        token_values,
        query_gain,
        k_gain,
        norm_gain,
        expert_ids.T,
        gate_weights.T,
    )
    weights = (w_gate, w_up, w_down)
    weights = weights + tuple(exchange(w, 1) for w in weights)

    resid, far_rows, outgoing, info = [], [], [], None
    for c in range(chunks):
        residual, normed, outgoing, packed = attend(cache_len, arrays, outgoing, c, chunks, half, cap)
        info = packed if c == 0 else info
        resid.append(residual)
        far_rows.append(exchange(normed, ep // 2))
    far_info = exchange(info, ep // 2)
    near_back = around(expert(around(outgoing), weights))
    far_back = []
    for c in range(chunks):
        placed = around(relay(far_rows[c], far_info, c, half, cap))
        returned = around(expert(placed, weights))
        far_back.append(exchange(relay_back(returned, far_info, c, rows, cap), ep // 2))
    result = None
    for c in range(chunks):
        result = finish(resid[c], near_back, far_back[c], info, c, chunks, cap, result)
    return result


def solution(mesh):
    in_specs = (
        P(("grp", "ep"), None),
        P(("grp", "ep"), None),
        P(("grp", "ep"), None),
        P(("grp", "ep"), None),
        P(("grp", "ep"), None),
        P(("grp", "ep"), None),
        P(("grp", "ep")),
        P(),
        P(),
        P(),
        P(("grp", "ep"), None),
        P(("grp", "ep"), None),
        P(None, "ep"),
        P(None, "ep"),
        P("ep", None),
    )
    out_specs = P(("grp", "ep"), None)
    return jax.shard_map(local, mesh=mesh, in_specs=in_specs, out_specs=out_specs, check_vma=False)
```

```python
import math

import jax
import jax.numpy as jnp
from jax import lax
from jax.experimental import pallas as pl
from jax.experimental.pallas import tpu as pltpu
from jax.sharding import PartitionSpec as P

EPS = 1e-06
ROUTE = 128
MIB = 1 << 20
VMEM = pltpu.VMEM
SMEM = pltpu.SMEM


def exchange(value, distance):
    return lax.ppermute(value, "ep", [(i, i ^ distance) for i in range(lax.axis_size("ep"))])


def whole(array):
    return pl.BlockSpec(array.shape, lambda: (0,) * array.ndim, memory_space=VMEM)


def params(mib):
    return pltpu.CompilerParams(vmem_limit_bytes=mib * MIB)


def unread(arrays):
    return [pl.BlockSpec(memory_space=pl.ANY)] * len(arrays)


def taking(microseconds):
    return pl.CostEstimate(flops=1, bytes_accessed=int(microseconds * 3.5e6), transcendentals=0)


def slots_of(half, cap):
    chip = lax.axis_index("ep") // 2
    lane = lax.broadcasted_iota(jnp.int32, (half * cap, 1), 0)
    apart = lane // cap
    position = chip & (half - 1)
    expert = (chip - position) + (apart ^ position)
    return expert.astype(jnp.float32), (lane - apart * cap).astype(jnp.float32)


def slot_hits(info, expert, slot):
    width, rows = info.shape
    named = info[0:1, :] == expert
    for k in range(1, width // 2):
        named = jnp.logical_or(named, info[k : k + 1, :] == expert)
    row = lax.broadcasted_iota(jnp.int32, (rows, rows), 0)
    col = lax.broadcasted_iota(jnp.int32, (rows, rows), 1)
    earlier = jnp.where(row < col, 1.0, 0.0).astype(jnp.bfloat16)
    ones = jnp.where(named, 1.0, 0.0)
    rank = jnp.dot(ones.astype(jnp.bfloat16), earlier, preferred_element_type=jnp.float32)
    return jnp.where(rank == slot, ones, 0.0)


def route_lanes(top, width):
    row = lax.broadcasted_iota(jnp.int32, (2 * top, width), 0)
    lane = lax.broadcasted_iota(jnp.int32, (2 * top, width), 1)
    apart = lane - row
    gate = row >= top
    later = jnp.logical_and(gate, jnp.logical_or(apart == top, apart == 2 * top))
    return jnp.where(jnp.logical_or(apart == 0, later), 1.0, 0.0).astype(jnp.bfloat16)


def pack_route(info, width):
    top = info.shape[0] // 2
    gates = info[top:, :]
    high = gates.astype(jnp.bfloat16).astype(jnp.float32)
    middle = (gates - high).astype(jnp.bfloat16).astype(jnp.float32)
    low = gates - high - middle
    parts = jnp.concatenate([info[:top, :], high, middle, low], axis=0).astype(jnp.bfloat16)
    row = lax.broadcasted_iota(jnp.int32, (4 * top, width), 0)
    lane = lax.broadcasted_iota(jnp.int32, (4 * top, width), 1)
    place = jnp.where(row == lane, 1.0, 0.0).astype(jnp.bfloat16)
    return lax.dot_general(parts, place, (((0,), (0,)), ((), ())), preferred_element_type=jnp.float32).astype(
        jnp.bfloat16
    )


def unpack_route(lanes, top):
    return lax.dot_general(
        route_lanes(top, lanes.shape[1]), lanes, (((1,), (1,)), ((), ())), preferred_element_type=jnp.float32
    )


def spread_rows(info, rows_bf16, out_refs, cap):
    half = len(out_refs)
    expert, slot = slots_of(half, cap)
    hits = slot_hits(info, expert, slot).astype(jnp.bfloat16)
    placed = jnp.dot(hits, rows_bf16, preferred_element_type=jnp.float32).astype(jnp.bfloat16)
    for d in range(half):
        out_refs[d][...] = placed[d * cap : (d + 1) * cap, :]


def weighted_rows(info, half, joined, cap):
    top = info.shape[0] // 2
    expert, slot = slots_of(half, cap)
    hits = slot_hits(info, expert, slot)
    weight = jnp.zeros_like(hits)
    for k in range(top):
        weight = weight + jnp.where(info[k : k + 1, :] == expert, info[top + k : top + k + 1, :], 0.0)
    weight = weight * hits
    high = weight.astype(jnp.bfloat16)
    low = (weight - high.astype(jnp.float32)).astype(jnp.bfloat16)
    values = joined[...]
    first = (((0,), (0,)), ((), ()))
    return lax.dot_general(high, values, first, preferred_element_type=jnp.float32) + lax.dot_general(
        low, values, first, preferred_element_type=jnp.float32
    )


def unit_rows(values, gain):
    return values * lax.rsqrt(jnp.mean(values * values, axis=-1, keepdims=True) + EPS) * gain


def attend(cache_len, arrays, before, chunk, chunks, half, cap):
    queries, hidden_in, stored_keys, stored_values, token_keys, token_values = arrays[:6]
    ids, gates = arrays[9:]
    rows, width = hidden_in.shape[0] // chunks, hidden_in.shape[1]
    cache_rows, kv_width = stored_keys.shape
    token_rows = token_keys.shape[0]
    head = arrays[6].shape[0]
    heads_kv = kv_width // head
    heads = width // head
    group = heads // heads_kv
    keys = cache_rows + token_rows
    top = ids.shape[0]
    first, last = chunk == 0, chunk == chunks - 1
    mine = pl.ds(chunk * rows, rows)
    per = max(1, min(group, 256 // rows))
    block = per * rows
    near_rows = cap * chunks if last else cap
    out_shape = [
        jax.ShapeDtypeStruct((rows, width), jnp.float32),
        jax.ShapeDtypeStruct((rows, width + ROUTE), jnp.bfloat16),
    ]
    out_shape += [jax.ShapeDtypeStruct((near_rows, width), jnp.bfloat16)] * half
    if first:
        out_shape.append(jax.ShapeDtypeStruct((2 * top, token_rows), jnp.float32))

    def body(len_ref, *refs):
        hbm, refs = refs[:11], refs[11:]
        carried, refs = refs[: len(before)], refs[len(before) :]
        outs, scratch = refs[: len(out_shape)], refs[len(out_shape) :]
        (q_ref, hid_ref, sk_ref, sv_ref, tk_ref, tv_ref, qg_ref, kg_ref, ng_ref, ids_ref, gates_ref) = scratch[:11]
        kn_ref, vx_ref, qs_ref, info_ref, sems = scratch[11:]
        resid_ref, normed_ref, out_refs = outs[0], outs[1], outs[2 : 2 + half]
        copies = []
        for i in range(11):
            source = hbm[i].at[mine, :] if i < 2 else hbm[i]
            target = scratch[i].at[0] if 6 <= i < 9 else scratch[i]
            copies.append(pltpu.make_async_copy(source, target, sems.at[i]))
        order = (2, 7, 4, 0, 6, 3, 5, 9, 10, 1, 8)
        for i in order:
            copies[i].start()
        length = len_ref[0]
        live = lax.broadcasted_iota(jnp.int32, (cache_rows, head), 0) < length
        live_ones = jnp.where(live, 1.0, 0.0).astype(jnp.bfloat16)
        for i in (2, 7, 4):
            copies[i].wait()
        k_gain = kg_ref[...]
        for g in range(heads_kv):
            cols = slice(g * head, (g + 1) * head)
            kn_ref[g, :cache_rows, :] = unit_rows(sk_ref[:, cols].astype(jnp.float32), k_gain).astype(jnp.bfloat16)
            kn_ref[g, cache_rows:, :] = unit_rows(tk_ref[:, cols].astype(jnp.float32), k_gain).astype(jnp.bfloat16)
        for i in (0, 6):
            copies[i].wait()
        q_gain = qg_ref[...] * (math.log2(math.e) / math.sqrt(head))
        for h in range(heads):
            x = q_ref[:, h * head : (h + 1) * head].astype(jnp.float32)
            qs_ref[h * rows : (h + 1) * rows, :] = unit_rows(x, q_gain).astype(jnp.bfloat16)
        for i in (3, 5):
            copies[i].wait()
        for g in range(heads_kv):
            cols = slice(g * head, (g + 1) * head)
            vx_ref[g, :cache_rows, :head] = jnp.where(live, sv_ref[:, cols].astype(jnp.float32), 0.0).astype(
                jnp.bfloat16
            )
            vx_ref[g, :cache_rows, head:] = live_ones
            vx_ref[g, cache_rows:, :head] = tv_ref[:, cols]
            vx_ref[g, cache_rows:, head:] = jnp.ones((token_rows, head), jnp.bfloat16)
        for i in (9, 10, 1, 8):
            copies[i].wait()
        info_ref[:top, :] = ids_ref[...].astype(jnp.float32)
        info_ref[top:, :] = gates_ref[...]
        if first:
            outs[-1][...] = info_ref[...]
        own = lax.broadcasted_iota(jnp.int32, (block, token_rows), 0) % rows + chunk * rows
        causal = lax.broadcasted_iota(jnp.int32, (block, token_rows), 1) <= own
        square = jnp.zeros((rows, head), jnp.float32)
        last_dims = (((1,), (1,)), ((), ()))
        for b in range(heads // per):
            g = b * per // group
            q_block = qs_ref[b * block : (b + 1) * block, :]
            scores = lax.dot_general(q_block, kn_ref[g, :cache_rows, :], last_dims, preferred_element_type=jnp.float32)
            raised = jnp.exp2(scores).astype(jnp.bfloat16)
            scores_new = lax.dot_general(
                q_block, kn_ref[g, cache_rows:, :], last_dims, preferred_element_type=jnp.float32
            )
            raised_new = jnp.where(causal, jnp.exp2(scores_new), 0.0).astype(jnp.bfloat16)
            summed = jnp.dot(raised, vx_ref[g, :cache_rows, :], preferred_element_type=jnp.float32) + jnp.dot(
                raised_new, vx_ref[g, cache_rows:, :], preferred_element_type=jnp.float32
            )
            attended = (summed[:, :head] / summed[:, head:]).astype(jnp.bfloat16).astype(jnp.float32)
            for i in range(per):
                cols = slice((b * per + i) * head, (b * per + i + 1) * head)
                resid = hid_ref[:, cols].astype(jnp.float32) + attended[i * rows : (i + 1) * rows, :]
                resid_ref[:, cols] = resid
                square = square + resid * resid
        scale = lax.rsqrt(jnp.sum(square, axis=-1, keepdims=True) / width + EPS)
        normed = (resid_ref[...] * scale * ng_ref[...]).astype(jnp.bfloat16)
        route = info_ref[:, chunk * rows : (chunk + 1) * rows]
        normed_ref[:, :width] = normed
        normed_ref[:, width:] = pack_route(route, ROUTE)
        tail = slice(near_rows - cap, near_rows)
        spread_rows(route, normed, [o.at[tail, :] for o in out_refs], cap)
        for i in range(len(before)):
            out_refs[i][: near_rows - cap, :] = carried[i][...]

    results = pl.pallas_call(
        body,
        out_shape=out_shape,
        in_specs=[pl.BlockSpec(memory_space=SMEM)]
        + [pl.BlockSpec(memory_space=pltpu.HBM)] * 11
        + [whole(b) for b in before],
        out_specs=[whole(o) for o in out_shape],
        scratch_shapes=[
            VMEM((rows, width), jnp.bfloat16),
            VMEM((rows, width), jnp.bfloat16),
            VMEM((cache_rows, kv_width), jnp.bfloat16),
            VMEM((cache_rows, kv_width), jnp.bfloat16),
            VMEM((token_rows, kv_width), jnp.bfloat16),
            VMEM((token_rows, kv_width), jnp.bfloat16),
            VMEM((1, head), jnp.float32),
            VMEM((1, head), jnp.float32),
            VMEM((1, width), jnp.float32),
            VMEM((top, token_rows), jnp.int32),
            VMEM((top, token_rows), jnp.float32),
            VMEM((heads_kv, keys, head), jnp.bfloat16),
            VMEM((heads_kv, keys, 2 * head), jnp.bfloat16),
            VMEM((rows * heads, head), jnp.bfloat16),
            VMEM((2 * top, token_rows), jnp.float32),
            pltpu.SemaphoreType.DMA((11,)),
        ],
        compiler_params=params(24),
        cost_estimate=taking(4),
        name="attend",
    )(cache_len, *arrays, *before)
    return results[0], results[1], list(results[2 : 2 + half]), (results[-1] if first else None)


def relay(rows_in, top, half, cap, carried, after):
    width = rows_in.shape[1] - ROUTE
    out = [jax.ShapeDtypeStruct((cap, width), jnp.bfloat16)] * half
    out += [jax.ShapeDtypeStruct(x.shape, x.dtype) for x in carried]

    def body(rows_ref, *refs):
        outs = refs[len(carried) + len(after) :]
        spread_rows(unpack_route(rows_ref[:, width:], top), rows_ref[:, :width], outs[:half], cap)
        for i in range(len(carried)):
            outs[half + i][...] = refs[i][...]

    results = pl.pallas_call(
        body,
        out_shape=out,
        in_specs=[whole(rows_in)] + [whole(x) for x in carried] + unread(after),
        out_specs=[whole(o) for o in out],
        compiler_params=params(24),
        cost_estimate=taking(0.5),
        name="relay",
    )(rows_in, *carried, *after)
    return list(results[:half]), list(results[half:])


def arrange(arrays, plan, after):
    width = arrays[0].shape[1]
    out = [jax.ShapeDtypeStruct((sum(piece[2] for piece in pieces), width), arrays[0].dtype) for pieces in plan]

    def body(*refs):
        outs = refs[len(arrays) + len(after) :]
        for out_ref, pieces in zip(outs, plan):
            at = 0
            for index, start, count in pieces:
                out_ref[at : at + count, :] = refs[index][start : start + count, :]
                at += count

    return list(
        pl.pallas_call(
            body,
            out_shape=out,
            in_specs=[whole(x) for x in arrays] + unread(after),
            out_specs=[whole(x) for x in out],
            compiler_params=params(24),
            cost_estimate=taking(0.3),
            name="arrange",
        )(*arrays, *after)
    )


def expert(ins, weights, outs, after, microseconds):
    rows, width = ins[0].shape
    total = len(ins) * rows
    hidden = weights[0].shape[1]
    block = min(total, 128)
    part = 512
    back = total // outs
    out = [jax.ShapeDtypeStruct((back, width), jnp.bfloat16)] * outs

    def body(*refs):
        in_refs, refs = refs[: len(ins)], refs[len(ins) :]
        (wg0, wu0, wd0, wg1, wu1, wd1), refs = refs[:6], refs[6 + len(after) :]
        out_refs, (x_ref, y_ref) = refs[:outs], refs[outs:]
        for i in range(len(ins)):
            x_ref[i * rows : (i + 1) * rows, :] = in_refs[i][...]

        def rows_of(span):
            inners = []
            for wg, wu in ((wg0, wu0), (wg1, wu1)):
                pre = jnp.zeros((block, 2 * hidden), jnp.float32)
                for k in range(0, width, part):
                    both = jnp.concatenate([wg[k : k + part, :], wu[k : k + part, :]], axis=1)
                    pre = pre + jnp.dot(x_ref[span, k : k + part], both, preferred_element_type=jnp.float32)
                gate = pre[:, :hidden]
                inners.append((gate / (1.0 + jnp.exp(-gate)) * pre[:, hidden:]).astype(jnp.bfloat16))
            inner = jnp.concatenate(inners, axis=1)
            for k in range(0, width, part):
                down = jnp.concatenate([wd0[:, k : k + part], wd1[:, k : k + part]], axis=0)
                y_ref[span, k : k + part] = jnp.dot(inner, down, preferred_element_type=jnp.float32).astype(
                    jnp.bfloat16
                )

        if total == block:
            rows_of(slice(0, block))
        else:

            @pl.loop(0, total // block)
            def _(r):
                rows_of(pl.ds(pl.multiple_of(r * block, block), block))

        for i in range(outs):
            out_refs[i][...] = y_ref[i * back : (i + 1) * back, :]

    return list(
        pl.pallas_call(
            body,
            out_shape=out,
            in_specs=[whole(x) for x in ins] + [whole(w) for w in weights] + unread(after),
            out_specs=[whole(o) for o in out],
            scratch_shapes=[VMEM((total, width), jnp.bfloat16)] * 2,
            compiler_params=params(24),
            cost_estimate=taking(microseconds),
            name="expert",
        )(*ins, *weights, *after)
    )


def relay_back(returned, rows_in, top, cap, after):
    half = len(returned)
    rows, width = rows_in.shape[0], returned[0].shape[1]
    out = jax.ShapeDtypeStruct((rows, width), jnp.bfloat16)

    def body(rows_ref, *refs):
        in_refs, (out_ref, joined) = refs[:half], refs[half + len(after) :]
        for d in range(half):
            joined[d * cap : (d + 1) * cap, :] = in_refs[d][...]
        far = weighted_rows(unpack_route(rows_ref[:, width:], top), half, joined, cap)
        out_ref[...] = far.astype(jnp.bfloat16)

    return pl.pallas_call(
        body,
        out_shape=out,
        in_specs=[whole(rows_in)] + [whole(returned[0])] * half + unread(after),
        out_specs=whole(out),
        scratch_shapes=[VMEM((half * cap, width), jnp.bfloat16)],
        compiler_params=params(24),
        cost_estimate=taking(0.6),
        name="relay_back",
    )(rows_in, *returned, *after)


def finish(resid, far, returned, info, cap):
    half = len(returned)
    chunks = len(resid)
    rows, width = resid[0].shape
    out = jax.ShapeDtypeStruct((rows * chunks, width), jnp.bfloat16)

    def body(info_ref, *refs):
        resid_refs, far_refs, refs = refs[:chunks], refs[chunks : 2 * chunks], refs[2 * chunks :]
        in_refs, (out_ref, joined) = refs[:half], refs[half:]
        for c in range(chunks):
            for d in range(half):
                joined[d * cap : (d + 1) * cap, :] = in_refs[d][c * cap : (c + 1) * cap, :]
            near = weighted_rows(info_ref[:, c * rows : (c + 1) * rows], half, joined, cap)
            out_ref[c * rows : (c + 1) * rows, :] = (
                resid_refs[c][...] + (near + far_refs[c][...].astype(jnp.float32))
            ).astype(jnp.bfloat16)

    return pl.pallas_call(
        body,
        out_shape=out,
        in_specs=[whole(x) for x in (info, *resid, *far, *returned)],
        out_specs=whole(out),
        scratch_shapes=[VMEM((half * cap, width), jnp.bfloat16)],
        compiler_params=params(24),
        cost_estimate=taking(2),
        name="finish",
    )(info, *resid, *far, *returned)


def around(parts):
    moved = {d: exchange(parts[d], 2 * d) for d in reversed(range(1, len(parts)))}
    return [parts[0]] + [moved[d] for d in range(1, len(parts))]


def local(
    hidden_in,
    queries,
    token_keys,
    token_values,
    stored_keys,
    stored_values,
    cache_len,
    query_gain,
    k_gain,
    norm_gain,
    expert_ids,
    gate_weights,
    w_gate,
    w_up,
    w_down,
):
    token_rows, top = expert_ids.shape
    ep = lax.axis_size("ep")
    experts = ep // 2
    half = experts // 2
    slots = 2 * token_rows * top // experts
    chunks = 2 if slots >= 32 else 1
    cap = slots // chunks
    rows = token_rows // chunks
    arrays = (
        queries,
        hidden_in,
        stored_keys,
        stored_values,
        token_keys,
        token_values,
        query_gain,
        k_gain,
        norm_gain,
        expert_ids.T,
        gate_weights.T,
    )
    arrays = tuple(pltpu.with_memory_space_constraint(x, pltpu.HBM) for x in arrays)
    weights = (w_gate, w_up, w_down)
    weights = weights + tuple(exchange(w, 1) for w in weights)

    resid, normed, outgoing, info = [], [], [], None
    for c in range(chunks):
        residual, rows_c, outgoing, packed = attend(cache_len, arrays, outgoing, c, chunks, half, cap)
        info = packed if c == 0 else info
        resid.append(residual)
        normed.append(rows_c)
    far_rows = [exchange(x, ep // 2) for x in normed]
    near = around(arrange(outgoing, [[(d, 0, slots)] for d in range(half)], list(weights[3:])))
    placed = [around(relay(far_rows[0], top, half, cap, [], [])[0])]
    after = near[1:]
    for c in range(1, chunks):
        arrived, _ = relay(far_rows[c], top, half, cap, [], after)
        placed.append(around(arrived))
        after = [arrived[0]]
    near_out = expert(near, weights, half, after, 4)
    after = near_out[0]
    returned, far_back = [], []
    for c in range(chunks):
        far_out = expert(placed[c], weights, half, [after], 0.01)
        returned.append(around(far_out))
        after = far_out[0]
    for c in range(chunks):
        back = relay_back(returned[c], far_rows[c], top, cap, [after] + far_back)
        far_back.append(exchange(back, ep // 2))
        after = back
    return finish(resid, far_back, around(near_out), info, cap)


def solution(mesh):
    in_specs = (
        P(("grp", "ep"), None),
        P(("grp", "ep"), None),
        P(("grp", "ep"), None),
        P(("grp", "ep"), None),
        P(("grp", "ep"), None),
        P(("grp", "ep"), None),
        P(("grp", "ep")),
        P(),
        P(),
        P(),
        P(("grp", "ep"), None),
        P(("grp", "ep"), None),
        P(None, "ep"),
        P(None, "ep"),
        P("ep", None),
    )
    out_specs = P(("grp", "ep"), None)
    return jax.shard_map(local, mesh=mesh, in_specs=in_specs, out_specs=out_specs, check_vma=False)
```

```python
import math

import jax
import jax.numpy as jnp
from jax import lax
from jax.experimental import pallas as pl
from jax.experimental.pallas import tpu as pltpu
from jax.sharding import PartitionSpec as P

EPS = 1e-06
ROUTE = 128
MIB = 1 << 20
VMEM = pltpu.VMEM
SMEM = pltpu.SMEM


def exchange(value, distance):
    return lax.ppermute(value, "ep", [(i, i ^ distance) for i in range(lax.axis_size("ep"))])


def whole(array):
    return pl.BlockSpec(array.shape, lambda: (0,) * array.ndim, memory_space=VMEM)


def params(mib):
    return pltpu.CompilerParams(vmem_limit_bytes=mib * MIB)


def unread(arrays):
    return [pl.BlockSpec(memory_space=pl.ANY)] * len(arrays)


def taking(microseconds):
    return pl.CostEstimate(flops=1, bytes_accessed=int(microseconds * 3.5e6), transcendentals=0)


def slots_of(half, cap):
    chip = lax.axis_index("ep") // 2
    lane = lax.broadcasted_iota(jnp.int32, (half * cap, 1), 0)
    apart = lane // cap
    position = chip & (half - 1)
    expert = (chip - position) + (apart ^ position)
    return expert.astype(jnp.float32), (lane - apart * cap).astype(jnp.float32)


def slot_hits(info, expert, slot):
    width, rows = info.shape
    named = info[0:1, :] == expert
    for k in range(1, width // 2):
        named = jnp.logical_or(named, info[k : k + 1, :] == expert)
    row = lax.broadcasted_iota(jnp.int32, (rows, rows), 0)
    col = lax.broadcasted_iota(jnp.int32, (rows, rows), 1)
    earlier = jnp.where(row < col, 1.0, 0.0).astype(jnp.bfloat16)
    ones = jnp.where(named, 1.0, 0.0)
    rank = jnp.dot(ones.astype(jnp.bfloat16), earlier, preferred_element_type=jnp.float32)
    return jnp.where(rank == slot, ones, 0.0)


def route_lanes(top, width):
    row = lax.broadcasted_iota(jnp.int32, (2 * top, width), 0)
    lane = lax.broadcasted_iota(jnp.int32, (2 * top, width), 1)
    apart = lane - row
    gate = row >= top
    later = jnp.logical_and(gate, jnp.logical_or(apart == top, apart == 2 * top))
    return jnp.where(jnp.logical_or(apart == 0, later), 1.0, 0.0).astype(jnp.bfloat16)


def pack_route(info, width):
    top = info.shape[0] // 2
    gates = info[top:, :]
    high = gates.astype(jnp.bfloat16).astype(jnp.float32)
    middle = (gates - high).astype(jnp.bfloat16).astype(jnp.float32)
    low = gates - high - middle
    parts = jnp.concatenate([info[:top, :], high, middle, low], axis=0).astype(jnp.bfloat16)
    row = lax.broadcasted_iota(jnp.int32, (4 * top, width), 0)
    lane = lax.broadcasted_iota(jnp.int32, (4 * top, width), 1)
    place = jnp.where(row == lane, 1.0, 0.0).astype(jnp.bfloat16)
    return lax.dot_general(parts, place, (((0,), (0,)), ((), ())), preferred_element_type=jnp.float32).astype(
        jnp.bfloat16
    )


def unpack_route(lanes, top):
    return lax.dot_general(
        route_lanes(top, lanes.shape[1]), lanes, (((1,), (1,)), ((), ())), preferred_element_type=jnp.float32
    )


def spread_rows(info, rows_bf16, out_refs, cap):
    half = len(out_refs)
    expert, slot = slots_of(half, cap)
    hits = slot_hits(info, expert, slot).astype(jnp.bfloat16)
    placed = jnp.dot(hits, rows_bf16, preferred_element_type=jnp.float32).astype(jnp.bfloat16)
    for d in range(half):
        out_refs[d][...] = placed[d * cap : (d + 1) * cap, :]


def weighted_rows(info, half, joined, cap):
    top = info.shape[0] // 2
    expert, slot = slots_of(half, cap)
    hits = slot_hits(info, expert, slot)
    weight = jnp.zeros_like(hits)
    for k in range(top):
        weight = weight + jnp.where(info[k : k + 1, :] == expert, info[top + k : top + k + 1, :], 0.0)
    weight = weight * hits
    high = weight.astype(jnp.bfloat16)
    low = (weight - high.astype(jnp.float32)).astype(jnp.bfloat16)
    values = joined[...]
    first = (((0,), (0,)), ((), ()))
    return lax.dot_general(high, values, first, preferred_element_type=jnp.float32) + lax.dot_general(
        low, values, first, preferred_element_type=jnp.float32
    )


def unit_rows(values, gain, ones):
    square = jnp.dot((values * values).astype(jnp.bfloat16), ones, preferred_element_type=jnp.float32)
    return values * lax.rsqrt(square / values.shape[-1] + EPS) * gain


def attend(cache_len, arrays, before, chunk, chunks, half, cap):
    queries, hidden_in, stored_keys, stored_values, token_keys, token_values = arrays[:6]
    ids, gates = arrays[9:]
    rows, width = hidden_in.shape[0] // chunks, hidden_in.shape[1]
    cache_rows, kv_width = stored_keys.shape
    token_rows = token_keys.shape[0]
    head = arrays[6].shape[0]
    heads_kv = kv_width // head
    heads = width // head
    group = heads // heads_kv
    keys = cache_rows + token_rows
    top = ids.shape[0]
    first, last = chunk == 0, chunk == chunks - 1
    mine = pl.ds(chunk * rows, rows)
    per = max(1, min(group, 256 // rows))
    block = per * rows
    near_rows = cap * chunks if last else cap
    out_shape = [
        jax.ShapeDtypeStruct((rows, width), jnp.float32),
        jax.ShapeDtypeStruct((rows, width + ROUTE), jnp.bfloat16),
    ]
    out_shape += [jax.ShapeDtypeStruct((near_rows, width), jnp.bfloat16)] * half
    if first:
        out_shape.append(jax.ShapeDtypeStruct((2 * top, token_rows), jnp.float32))

    def body(len_hbm, *refs):
        hbm, refs = refs[:11], refs[11:]
        carried, refs = refs[: len(before)], refs[len(before) :]
        outs, scratch = refs[: len(out_shape)], refs[len(out_shape) :]
        (q_ref, hid_ref, sk_ref, sv_ref, tk_ref, tv_ref, qg_ref, kg_ref, ng_ref, ids_ref, gates_ref) = scratch[:11]
        kn_ref, vx_ref, qs_ref, info_ref, len_ref, sems = scratch[11:]
        resid_ref, normed_ref, out_refs = outs[0], outs[1], outs[2 : 2 + half]
        copies = []
        for i in range(11):
            source = hbm[i].at[mine, :] if i < 2 else hbm[i]
            target = scratch[i].at[0] if 6 <= i < 9 else scratch[i]
            copies.append(pltpu.make_async_copy(source, target, sems.at[i]))
        copies.append(pltpu.make_async_copy(len_hbm, len_ref, sems.at[11]))
        for i in (0, 6, 11, 2, 7, 4, 3, 5, 9, 10, 1, 8):
            copies[i].start()
        ones = jnp.ones((head, head), jnp.bfloat16)
        for i in (0, 6):
            copies[i].wait()
        q_gain = qg_ref[...] * (math.log2(math.e) / math.sqrt(head))
        for h in range(heads):
            x = q_ref[:, h * head : (h + 1) * head].astype(jnp.float32)
            qs_ref[h * rows : (h + 1) * rows, :] = unit_rows(x, q_gain, ones).astype(jnp.bfloat16)
        for i in (2, 7, 4):
            copies[i].wait()
        k_gain = kg_ref[...]
        for g in range(heads_kv):
            cols = slice(g * head, (g + 1) * head)
            kn_ref[g, :cache_rows, :] = unit_rows(sk_ref[:, cols].astype(jnp.float32), k_gain, ones).astype(
                jnp.bfloat16
            )
            kn_ref[g, cache_rows:, :] = unit_rows(tk_ref[:, cols].astype(jnp.float32), k_gain, ones).astype(
                jnp.bfloat16
            )
        for i in (11, 3, 5):
            copies[i].wait()
        live = lax.broadcasted_iota(jnp.int32, (cache_rows, head), 0) < len_ref[0]
        live_ones = jnp.where(live, 1.0, 0.0).astype(jnp.bfloat16)
        for g in range(heads_kv):
            cols = slice(g * head, (g + 1) * head)
            vx_ref[g, :cache_rows, :head] = sv_ref[:, cols] * live_ones
            vx_ref[g, :cache_rows, head:] = live_ones
            vx_ref[g, cache_rows:, :head] = tv_ref[:, cols]
            vx_ref[g, cache_rows:, head:] = jnp.ones((token_rows, head), jnp.bfloat16)
        for i in (9, 10, 1, 8):
            copies[i].wait()
        info_ref[:top, :] = ids_ref[...].astype(jnp.float32)
        info_ref[top:, :] = gates_ref[...]
        if first:
            outs[-1][...] = info_ref[...]
        own = lax.broadcasted_iota(jnp.int32, (block, token_rows), 0) % rows + chunk * rows
        causal = lax.broadcasted_iota(jnp.int32, (block, token_rows), 1) <= own
        square = jnp.zeros((rows, head), jnp.float32)
        last_dims = (((1,), (1,)), ((), ()))
        for b in range(heads // per):
            g = b * per // group
            q_block = qs_ref[b * block : (b + 1) * block, :]
            scores = lax.dot_general(q_block, kn_ref[g, :cache_rows, :], last_dims, preferred_element_type=jnp.float32)
            raised = jnp.exp2(scores).astype(jnp.bfloat16)
            scores_new = lax.dot_general(
                q_block, kn_ref[g, cache_rows:, :], last_dims, preferred_element_type=jnp.float32
            )
            raised_new = jnp.where(causal, jnp.exp2(scores_new), 0.0).astype(jnp.bfloat16)
            summed = jnp.dot(raised, vx_ref[g, :cache_rows, :], preferred_element_type=jnp.float32) + jnp.dot(
                raised_new, vx_ref[g, cache_rows:, :], preferred_element_type=jnp.float32
            )
            attended = (summed[:, :head] / summed[:, head:]).astype(jnp.bfloat16).astype(jnp.float32)
            for i in range(per):
                cols = slice((b * per + i) * head, (b * per + i + 1) * head)
                resid = hid_ref[:, cols].astype(jnp.float32) + attended[i * rows : (i + 1) * rows, :]
                resid_ref[:, cols] = resid
                square = square + resid * resid
        scale = lax.rsqrt(jnp.sum(square, axis=-1, keepdims=True) / width + EPS)
        normed = (resid_ref[...] * scale * ng_ref[...]).astype(jnp.bfloat16)
        route = info_ref[:, chunk * rows : (chunk + 1) * rows]
        normed_ref[:, :width] = normed
        normed_ref[:, width:] = pack_route(route, ROUTE)
        tail = slice(near_rows - cap, near_rows)
        spread_rows(route, normed, [o.at[tail, :] for o in out_refs], cap)
        for i in range(len(before)):
            out_refs[i][: near_rows - cap, :] = carried[i][...]

    results = pl.pallas_call(
        body,
        out_shape=out_shape,
        in_specs=[pl.BlockSpec(memory_space=pl.ANY)]
        + [pl.BlockSpec(memory_space=pltpu.HBM)] * 11
        + [whole(b) for b in before],
        out_specs=[whole(o) for o in out_shape],
        scratch_shapes=[
            VMEM((rows, width), jnp.bfloat16),
            VMEM((rows, width), jnp.bfloat16),
            VMEM((cache_rows, kv_width), jnp.bfloat16),
            VMEM((cache_rows, kv_width), jnp.bfloat16),
            VMEM((token_rows, kv_width), jnp.bfloat16),
            VMEM((token_rows, kv_width), jnp.bfloat16),
            VMEM((1, head), jnp.float32),
            VMEM((1, head), jnp.float32),
            VMEM((1, width), jnp.float32),
            VMEM((top, token_rows), jnp.int32),
            VMEM((top, token_rows), jnp.float32),
            VMEM((heads_kv, keys, head), jnp.bfloat16),
            VMEM((heads_kv, keys, 2 * head), jnp.bfloat16),
            VMEM((rows * heads, head), jnp.bfloat16),
            VMEM((2 * top, token_rows), jnp.float32),
            SMEM((1,), jnp.int32),
            pltpu.SemaphoreType.DMA((12,)),
        ],
        compiler_params=params(24),
        cost_estimate=taking(4),
        name="attend",
    )(cache_len, *arrays, *before)
    return results[0], results[1], list(results[2 : 2 + half]), (results[-1] if first else None)


def relay(rows_in, top, half, cap, carried, after, microseconds):
    width = rows_in.shape[1] - ROUTE
    out = [jax.ShapeDtypeStruct((cap, width), jnp.bfloat16)] * half
    out += [jax.ShapeDtypeStruct(x.shape, x.dtype) for x in carried]

    def body(rows_ref, *refs):
        outs = refs[len(carried) + len(after) :]
        spread_rows(unpack_route(rows_ref[:, width:], top), rows_ref[:, :width], outs[:half], cap)
        for i in range(len(carried)):
            outs[half + i][...] = refs[i][...]

    results = pl.pallas_call(
        body,
        out_shape=out,
        in_specs=[whole(rows_in)] + [whole(x) for x in carried] + unread(after),
        out_specs=[whole(o) for o in out],
        compiler_params=params(24),
        cost_estimate=taking(microseconds),
        name="relay",
    )(rows_in, *carried, *after)
    return list(results[:half]), list(results[half:])


def passed(arrays, after, microseconds):
    def body(*refs):
        outs = refs[len(arrays) + len(after) :]
        for i in range(len(arrays)):
            outs[i][...] = refs[i][...]

    return list(
        pl.pallas_call(
            body,
            out_shape=[jax.ShapeDtypeStruct(x.shape, x.dtype) for x in arrays],
            in_specs=[whole(x) for x in arrays] + unread(after),
            out_specs=[whole(x) for x in arrays],
            compiler_params=params(24),
            cost_estimate=taking(microseconds),
            name="passed",
        )(*arrays, *after)
    )


def expert(ins, weights, outs, after, microseconds):
    rows, width = ins[0].shape
    total = len(ins) * rows
    hidden = weights[0].shape[1]
    block = min(total, 128)
    part = 1024
    back = total // outs
    out = [jax.ShapeDtypeStruct((back, width), jnp.bfloat16)] * outs

    def body(*refs):
        in_refs, refs = refs[: len(ins)], refs[len(ins) :]
        (wg0, wu0, wd0, wg1, wu1, wd1), refs = refs[:6], refs[6 + len(after) :]
        out_refs, (x_ref, y_ref) = refs[:outs], refs[outs:]
        for i in range(len(ins)):
            x_ref[i * rows : (i + 1) * rows, :] = in_refs[i][...]

        def rows_of(span):
            inners = []
            for wg, wu in ((wg0, wu0), (wg1, wu1)):
                both = jnp.concatenate([wg[...], wu[...]], axis=1)
                pre = jnp.dot(x_ref[span, :], both, preferred_element_type=jnp.float32)
                gate = pre[:, :hidden]
                inners.append((gate / (1.0 + jnp.exp(-gate)) * pre[:, hidden:]).astype(jnp.bfloat16))
            inner = jnp.concatenate(inners, axis=1)
            for k in range(0, width, part):
                down = jnp.concatenate([wd0[:, k : k + part], wd1[:, k : k + part]], axis=0)
                y_ref[span, k : k + part] = jnp.dot(inner, down, preferred_element_type=jnp.float32).astype(
                    jnp.bfloat16
                )

        if total == block:
            rows_of(slice(0, block))
        else:

            @pl.loop(0, total // block)
            def _(r):
                rows_of(pl.ds(pl.multiple_of(r * block, block), block))

        for i in range(outs):
            out_refs[i][...] = y_ref[i * back : (i + 1) * back, :]

    return list(
        pl.pallas_call(
            body,
            out_shape=out,
            in_specs=[whole(x) for x in ins] + [whole(w) for w in weights] + unread(after),
            out_specs=[whole(o) for o in out],
            scratch_shapes=[VMEM((total, width), jnp.bfloat16)] * 2,
            compiler_params=params(24),
            cost_estimate=taking(microseconds),
            name="expert",
        )(*ins, *weights, *after)
    )


def relay_back(returned, rows_in, top, cap, after, microseconds):
    half = len(returned)
    rows, width = rows_in.shape[0], returned[0].shape[1]
    out = jax.ShapeDtypeStruct((rows, width), jnp.bfloat16)

    def body(rows_ref, *refs):
        in_refs, (out_ref, joined) = refs[:half], refs[half + len(after) :]
        for d in range(half):
            joined[d * cap : (d + 1) * cap, :] = in_refs[d][...]
        far = weighted_rows(unpack_route(rows_ref[:, width:], top), half, joined, cap)
        out_ref[...] = far.astype(jnp.bfloat16)

    return pl.pallas_call(
        body,
        out_shape=out,
        in_specs=[whole(rows_in)] + [whole(returned[0])] * half + unread(after),
        out_specs=whole(out),
        scratch_shapes=[VMEM((half * cap, width), jnp.bfloat16)],
        compiler_params=params(24),
        cost_estimate=taking(microseconds),
        name="relay_back",
    )(rows_in, *returned, *after)


def add_near(resid, far, returned, info, cap, after, microseconds):
    half = len(returned)
    chunks = len(resid)
    rows, width = resid[0].shape
    out = jax.ShapeDtypeStruct((rows * chunks, width), jnp.float32)

    def body(info_ref, *refs):
        resid_refs, far_refs, refs = refs[:chunks], refs[chunks : chunks + len(far)], refs[chunks + len(far) :]
        in_refs, (out_ref, joined) = refs[:half], refs[half + len(after) :]
        for c in range(chunks):
            for d in range(half):
                joined[d * cap : (d + 1) * cap, :] = in_refs[d][c * cap : (c + 1) * cap, :]
            total = resid_refs[c][...] + weighted_rows(info_ref[:, c * rows : (c + 1) * rows], half, joined, cap)
            if c < len(far):
                total = total + far_refs[c][...].astype(jnp.float32)
            out_ref[c * rows : (c + 1) * rows, :] = total

    return pl.pallas_call(
        body,
        out_shape=out,
        in_specs=[whole(x) for x in (info, *resid, *far, *returned)] + unread(after),
        out_specs=whole(out),
        scratch_shapes=[VMEM((half * cap, width), jnp.bfloat16)],
        compiler_params=params(24),
        cost_estimate=taking(microseconds),
        name="add_near",
    )(info, *resid, *far, *returned, *after)


def add_far(base, far):
    total, width = base.shape
    first = total - far.shape[0]
    out = jax.ShapeDtypeStruct(base.shape, jnp.bfloat16)

    def body(base_ref, far_ref, out_ref):
        if first:
            out_ref[:first, :] = base_ref[:first, :].astype(jnp.bfloat16)
        out_ref[first:, :] = (base_ref[first:, :] + far_ref[...].astype(jnp.float32)).astype(jnp.bfloat16)

    return pl.pallas_call(
        body,
        out_shape=out,
        in_specs=[whole(base), whole(far)],
        out_specs=whole(out),
        compiler_params=params(24),
        cost_estimate=taking(1),
        name="add_far",
    )(base, far)


def around(parts):
    moved = {d: exchange(parts[d], 2 * d) for d in reversed(range(1, len(parts)))}
    return [parts[0]] + [moved[d] for d in range(1, len(parts))]


def local(
    hidden_in,
    queries,
    token_keys,
    token_values,
    stored_keys,
    stored_values,
    cache_len,
    query_gain,
    k_gain,
    norm_gain,
    expert_ids,
    gate_weights,
    w_gate,
    w_up,
    w_down,
):
    token_rows, top = expert_ids.shape
    ep = lax.axis_size("ep")
    experts = ep // 2
    half = experts // 2
    slots = 2 * token_rows * top // experts
    chunks = 2 if slots >= 32 else 1
    cap = slots // chunks
    rows = token_rows // chunks
    arrays = (
        queries,
        hidden_in,
        stored_keys,
        stored_values,
        token_keys,
        token_values,
        query_gain,
        k_gain,
        norm_gain,
        expert_ids.T,
        gate_weights.T,
    )
    arrays = tuple(pltpu.with_memory_space_constraint(x, pltpu.HBM) for x in arrays)
    weights = (w_gate, w_up, w_down)
    weights = weights + tuple(exchange(w, 1) for w in weights)

    resid, normed, outgoing, info = [], [], [], None
    for c in range(chunks):
        residual, rows_c, outgoing, packed = attend(cache_len, arrays, outgoing, c, chunks, half, cap)
        info = packed if c == 0 else info
        resid.append(residual)
        normed.append(rows_c)
    far_rows = [exchange(normed[0], ep // 2)]
    gate = passed(outgoing + normed[1:], list(weights[3:]), 0.3)
    near = around(gate[:half])
    far_rows += [exchange(x, ep // 2) for x in gate[half:]]

    placed = []
    after = [gate[0]]
    for c in range(chunks):
        slotted, _ = relay(far_rows[c], top, half, cap, [], after, 0.5)
        placed.append(around(slotted))
        after = [slotted[0], *near, placed[0][1]]
    returned, after = [], after[:1]
    for c in range(chunks):
        outs = expert(placed[c], weights, half, after, 0.01)
        returned.append(around(outs))
        after = outs[:1]
    far_back, near_out = [], None
    for c in range(chunks):
        if c == chunks - 1:
            near_out = expert(near, weights, half, after, 4)
            after = near_out[:1]
        back = relay_back(returned[c], far_rows[c], top, cap, after, 0.6)
        far_back.append(exchange(back, ep // 2))
        after = [back]
    near_back = around(passed(near_out, after, 0.1))
    base = add_near(resid, far_back[:-1], near_back, info, cap, [], 4)
    return add_far(base, far_back[-1])


def solution(mesh):
    in_specs = (
        P(("grp", "ep"), None),
        P(("grp", "ep"), None),
        P(("grp", "ep"), None),
        P(("grp", "ep"), None),
        P(("grp", "ep"), None),
        P(("grp", "ep"), None),
        P(("grp", "ep")),
        P(),
        P(),
        P(),
        P(("grp", "ep"), None),
        P(("grp", "ep"), None),
        P(None, "ep"),
        P(None, "ep"),
        P("ep", None),
    )
    out_specs = P(("grp", "ep"), None)
    return jax.shard_map(local, mesh=mesh, in_specs=in_specs, out_specs=out_specs, check_vma=False)
```

```python
import math

import jax
import jax.numpy as jnp
from jax import lax
from jax.experimental import pallas as pl
from jax.experimental.pallas import tpu as pltpu
from jax.sharding import PartitionSpec as P

EPS = 1e-06
ROUTE = 128
MIB = 1 << 20
VMEM = pltpu.VMEM
SMEM = pltpu.SMEM


def exchange(value, distance):
    return lax.ppermute(value, "ep", [(i, i ^ distance) for i in range(lax.axis_size("ep"))])


def whole(array):
    return pl.BlockSpec(array.shape, lambda: (0,) * array.ndim, memory_space=VMEM)


def params(mib):
    return pltpu.CompilerParams(vmem_limit_bytes=mib * MIB)


def unread(arrays):
    return [pl.BlockSpec(memory_space=pl.ANY)] * len(arrays)


def taking(microseconds):
    return pl.CostEstimate(flops=1, bytes_accessed=int(microseconds * 3.5e6), transcendentals=0)


def slots_of(half, cap):
    chip = lax.axis_index("ep") // 2
    lane = lax.broadcasted_iota(jnp.int32, (half * cap, 1), 0)
    apart = lane // cap
    position = chip & (half - 1)
    expert = (chip - position) + (apart ^ position)
    return expert.astype(jnp.float32), (lane - apart * cap).astype(jnp.float32)


def slot_hits(info, expert, slot):
    width, rows = info.shape
    named = info[0:1, :] == expert
    for k in range(1, width // 2):
        named = jnp.logical_or(named, info[k : k + 1, :] == expert)
    row = lax.broadcasted_iota(jnp.int32, (rows, rows), 0)
    col = lax.broadcasted_iota(jnp.int32, (rows, rows), 1)
    earlier = jnp.where(row < col, 1.0, 0.0).astype(jnp.bfloat16)
    ones = jnp.where(named, 1.0, 0.0)
    rank = jnp.dot(ones.astype(jnp.bfloat16), earlier, preferred_element_type=jnp.float32)
    return jnp.where(rank == slot, ones, 0.0)


def route_lanes(top, width):
    row = lax.broadcasted_iota(jnp.int32, (2 * top, width), 0)
    lane = lax.broadcasted_iota(jnp.int32, (2 * top, width), 1)
    apart = lane - row
    gate = row >= top
    later = jnp.logical_and(gate, jnp.logical_or(apart == top, apart == 2 * top))
    return jnp.where(jnp.logical_or(apart == 0, later), 1.0, 0.0).astype(jnp.bfloat16)


def pack_route(info, width):
    top = info.shape[0] // 2
    gates = info[top:, :]
    high = gates.astype(jnp.bfloat16).astype(jnp.float32)
    middle = (gates - high).astype(jnp.bfloat16).astype(jnp.float32)
    low = gates - high - middle
    parts = jnp.concatenate([info[:top, :], high, middle, low], axis=0).astype(jnp.bfloat16)
    row = lax.broadcasted_iota(jnp.int32, (4 * top, width), 0)
    lane = lax.broadcasted_iota(jnp.int32, (4 * top, width), 1)
    place = jnp.where(row == lane, 1.0, 0.0).astype(jnp.bfloat16)
    return lax.dot_general(parts, place, (((0,), (0,)), ((), ())), preferred_element_type=jnp.float32).astype(
        jnp.bfloat16
    )


def unpack_route(lanes, top):
    return lax.dot_general(
        route_lanes(top, lanes.shape[1]), lanes, (((1,), (1,)), ((), ())), preferred_element_type=jnp.float32
    )


def spread_rows(info, rows_bf16, out_refs, cap):
    half = len(out_refs)
    expert, slot = slots_of(half, cap)
    hits = slot_hits(info, expert, slot).astype(jnp.bfloat16)
    placed = jnp.dot(hits, rows_bf16, preferred_element_type=jnp.float32).astype(jnp.bfloat16)
    for d in range(half):
        out_refs[d][...] = placed[d * cap : (d + 1) * cap, :]


def weighted_rows(info, half, joined, cap):
    top = info.shape[0] // 2
    expert, slot = slots_of(half, cap)
    hits = slot_hits(info, expert, slot)
    weight = jnp.zeros_like(hits)
    for k in range(top):
        weight = weight + jnp.where(info[k : k + 1, :] == expert, info[top + k : top + k + 1, :], 0.0)
    weight = weight * hits
    high = weight.astype(jnp.bfloat16)
    low = (weight - high.astype(jnp.float32)).astype(jnp.bfloat16)
    values = joined[...]
    first = (((0,), (0,)), ((), ()))
    return lax.dot_general(high, values, first, preferred_element_type=jnp.float32) + lax.dot_general(
        low, values, first, preferred_element_type=jnp.float32
    )


def unit_rows(values, gain, ones):
    square = jnp.dot((values * values).astype(jnp.bfloat16), ones, preferred_element_type=jnp.float32)
    return values * lax.rsqrt(square / values.shape[-1] + EPS) * gain


def attend(cache_len, arrays, before, chunk, chunks, half, cap):
    queries, hidden_in, stored_keys, stored_values, token_keys, token_values = arrays[:6]
    ids, gates = arrays[9:]
    rows, width = hidden_in.shape[0] // chunks, hidden_in.shape[1]
    cache_rows, kv_width = stored_keys.shape
    token_rows = token_keys.shape[0]
    head = arrays[6].shape[0]
    heads_kv = kv_width // head
    heads = width // head
    group = heads // heads_kv
    keys = cache_rows + token_rows
    top = ids.shape[0]
    first, last = chunk == 0, chunk == chunks - 1
    mine = pl.ds(chunk * rows, rows)
    per = max(1, min(group, 256 // rows))
    block = per * rows
    near_rows = cap * chunks if last else cap
    out_shape = [
        jax.ShapeDtypeStruct((rows, width), jnp.float32),
        jax.ShapeDtypeStruct((rows, width + ROUTE), jnp.bfloat16),
    ]
    out_shape += [jax.ShapeDtypeStruct((near_rows, width), jnp.bfloat16)] * half
    if first:
        out_shape.append(jax.ShapeDtypeStruct((2 * top, token_rows), jnp.float32))

    def body(len_hbm, *refs):
        hbm, refs = refs[:11], refs[11:]
        carried, refs = refs[: len(before)], refs[len(before) :]
        outs, scratch = refs[: len(out_shape)], refs[len(out_shape) :]
        (q_ref, hid_ref, sk_ref, sv_ref, tk_ref, tv_ref, qg_ref, kg_ref, ng_ref, ids_ref, gates_ref) = scratch[:11]
        kn_ref, vx_ref, qs_ref, info_ref, len_ref, sems = scratch[11:]
        resid_ref, normed_ref, out_refs = outs[0], outs[1], outs[2 : 2 + half]
        copies = []
        for i in range(11):
            source = hbm[i].at[mine, :] if i < 2 else hbm[i]
            target = scratch[i].at[0] if 6 <= i < 9 else scratch[i]
            copies.append(pltpu.make_async_copy(source, target, sems.at[i]))
        copies.append(pltpu.make_async_copy(len_hbm, len_ref, sems.at[11]))
        for i in (0, 6, 11, 2, 7, 4, 3, 5, 9, 10, 1, 8):
            copies[i].start()
        ones = jnp.ones((head, head), jnp.bfloat16)
        for i in (0, 6):
            copies[i].wait()
        q_gain = qg_ref[...] * (math.log2(math.e) / math.sqrt(head))
        for h in range(heads):
            x = q_ref[:, h * head : (h + 1) * head].astype(jnp.float32)
            qs_ref[h * rows : (h + 1) * rows, :] = unit_rows(x, q_gain, ones).astype(jnp.bfloat16)
        for i in (2, 7, 4):
            copies[i].wait()
        k_gain = kg_ref[...]
        for g in range(heads_kv):
            cols = slice(g * head, (g + 1) * head)
            kn_ref[g, :cache_rows, :] = unit_rows(sk_ref[:, cols].astype(jnp.float32), k_gain, ones).astype(
                jnp.bfloat16
            )
            kn_ref[g, cache_rows:, :] = unit_rows(tk_ref[:, cols].astype(jnp.float32), k_gain, ones).astype(
                jnp.bfloat16
            )
        for i in (11, 3, 5):
            copies[i].wait()
        live = lax.broadcasted_iota(jnp.int32, (cache_rows, head), 0) < len_ref[0]
        live_ones = jnp.where(live, 1.0, 0.0).astype(jnp.bfloat16)
        for g in range(heads_kv):
            cols = slice(g * head, (g + 1) * head)
            vx_ref[g, :cache_rows, :head] = sv_ref[:, cols] * live_ones
            vx_ref[g, :cache_rows, head:] = live_ones
            vx_ref[g, cache_rows:, :head] = tv_ref[:, cols]
            vx_ref[g, cache_rows:, head:] = jnp.ones((token_rows, head), jnp.bfloat16)
        for i in (9, 10, 1, 8):
            copies[i].wait()
        info_ref[:top, :] = ids_ref[...].astype(jnp.float32)
        info_ref[top:, :] = gates_ref[...]
        if first:
            outs[-1][...] = info_ref[...]
        own = lax.broadcasted_iota(jnp.int32, (block, token_rows), 0) % rows + chunk * rows
        causal = lax.broadcasted_iota(jnp.int32, (block, token_rows), 1) <= own
        square = jnp.zeros((rows, head), jnp.float32)
        last_dims = (((1,), (1,)), ((), ()))
        for b in range(heads // per):
            g = b * per // group
            q_block = qs_ref[b * block : (b + 1) * block, :]
            scores = lax.dot_general(q_block, kn_ref[g, :cache_rows, :], last_dims, preferred_element_type=jnp.float32)
            raised = jnp.exp2(scores).astype(jnp.bfloat16)
            scores_new = lax.dot_general(
                q_block, kn_ref[g, cache_rows:, :], last_dims, preferred_element_type=jnp.float32
            )
            raised_new = jnp.where(causal, jnp.exp2(scores_new), 0.0).astype(jnp.bfloat16)
            summed = jnp.dot(raised, vx_ref[g, :cache_rows, :], preferred_element_type=jnp.float32) + jnp.dot(
                raised_new, vx_ref[g, cache_rows:, :], preferred_element_type=jnp.float32
            )
            attended = (summed[:, :head] / summed[:, head:]).astype(jnp.bfloat16).astype(jnp.float32)
            for i in range(per):
                cols = slice((b * per + i) * head, (b * per + i + 1) * head)
                resid = hid_ref[:, cols].astype(jnp.float32) + attended[i * rows : (i + 1) * rows, :]
                resid_ref[:, cols] = resid
                square = square + resid * resid
        scale = lax.rsqrt(jnp.sum(square, axis=-1, keepdims=True) / width + EPS)
        normed = (resid_ref[...] * scale * ng_ref[...]).astype(jnp.bfloat16)
        route = info_ref[:, chunk * rows : (chunk + 1) * rows]
        normed_ref[:, :width] = normed
        normed_ref[:, width:] = pack_route(route, ROUTE)
        tail = slice(near_rows - cap, near_rows)
        spread_rows(route, normed, [o.at[tail, :] for o in out_refs], cap)
        for i in range(len(before)):
            out_refs[i][: near_rows - cap, :] = carried[i][...]

    results = pl.pallas_call(
        body,
        out_shape=out_shape,
        in_specs=[pl.BlockSpec(memory_space=pl.ANY)]
        + [pl.BlockSpec(memory_space=pltpu.HBM)] * 11
        + [whole(b) for b in before],
        out_specs=[whole(o) for o in out_shape],
        scratch_shapes=[
            VMEM((rows, width), jnp.bfloat16),
            VMEM((rows, width), jnp.bfloat16),
            VMEM((cache_rows, kv_width), jnp.bfloat16),
            VMEM((cache_rows, kv_width), jnp.bfloat16),
            VMEM((token_rows, kv_width), jnp.bfloat16),
            VMEM((token_rows, kv_width), jnp.bfloat16),
            VMEM((1, head), jnp.float32),
            VMEM((1, head), jnp.float32),
            VMEM((1, width), jnp.float32),
            VMEM((top, token_rows), jnp.int32),
            VMEM((top, token_rows), jnp.float32),
            VMEM((heads_kv, keys, head), jnp.bfloat16),
            VMEM((heads_kv, keys, 2 * head), jnp.bfloat16),
            VMEM((rows * heads, head), jnp.bfloat16),
            VMEM((2 * top, token_rows), jnp.float32),
            SMEM((1,), jnp.int32),
            pltpu.SemaphoreType.DMA((12,)),
        ],
        compiler_params=params(24),
        cost_estimate=taking(4),
        name="attend",
    )(cache_len, *arrays, *before)
    return results[0], results[1], list(results[2 : 2 + half]), (results[-1] if first else None)


def relay(rows_in, top, half, cap, carried, after, microseconds):
    width = rows_in.shape[1] - ROUTE
    out = [jax.ShapeDtypeStruct((cap, width), jnp.bfloat16)] * half
    out += [jax.ShapeDtypeStruct(x.shape, x.dtype) for x in carried]

    def body(rows_ref, *refs):
        outs = refs[len(carried) + len(after) :]
        spread_rows(unpack_route(rows_ref[:, width:], top), rows_ref[:, :width], outs[:half], cap)
        for i in range(len(carried)):
            outs[half + i][...] = refs[i][...]

    results = pl.pallas_call(
        body,
        out_shape=out,
        in_specs=[whole(rows_in)] + [whole(x) for x in carried] + unread(after),
        out_specs=[whole(o) for o in out],
        compiler_params=params(24),
        cost_estimate=taking(microseconds),
        name="relay",
    )(rows_in, *carried, *after)
    return list(results[:half]), list(results[half:])


def passed(arrays, after, microseconds):
    def body(*refs):
        outs = refs[len(arrays) + len(after) :]
        for i in range(len(arrays)):
            outs[i][...] = refs[i][...]

    return list(
        pl.pallas_call(
            body,
            out_shape=[jax.ShapeDtypeStruct(x.shape, x.dtype) for x in arrays],
            in_specs=[whole(x) for x in arrays] + unread(after),
            out_specs=[whole(x) for x in arrays],
            compiler_params=params(24),
            cost_estimate=taking(microseconds),
            name="passed",
        )(*arrays, *after)
    )


def expert(ins, weights, outs, after, microseconds):
    rows, width = ins[0].shape
    total = len(ins) * rows
    hidden = weights[0].shape[1]
    block = 128
    held = -(-total // block) * block
    part = 1024
    back = total // outs
    out = [jax.ShapeDtypeStruct((back, width), jnp.bfloat16)] * outs

    def body(*refs):
        in_refs, refs = refs[: len(ins)], refs[len(ins) :]
        (wg0, wu0, wd0, wg1, wu1, wd1), refs = refs[:6], refs[6 + len(after) :]
        out_refs, (x_ref, y_ref) = refs[:outs], refs[outs:]
        for i in range(len(ins)):
            x_ref[i * rows : (i + 1) * rows, :] = in_refs[i][...]

        if held > total:
            x_ref[total:, :] = jnp.zeros((held - total, width), jnp.bfloat16)

        def rows_of(span):
            inners = []
            for wg, wu in ((wg0, wu0), (wg1, wu1)):
                both = jnp.concatenate([wg[...], wu[...]], axis=1)
                pre = jnp.dot(x_ref[span, :], both, preferred_element_type=jnp.float32)
                gate = pre[:, :hidden]
                inners.append((gate / (1.0 + jnp.exp(-gate)) * pre[:, hidden:]).astype(jnp.bfloat16))
            inner = jnp.concatenate(inners, axis=1)
            for k in range(0, width, part):
                down = jnp.concatenate([wd0[:, k : k + part], wd1[:, k : k + part]], axis=0)
                y_ref[span, k : k + part] = jnp.dot(inner, down, preferred_element_type=jnp.float32).astype(
                    jnp.bfloat16
                )

        if held == block:
            rows_of(slice(0, block))
        else:

            @pl.loop(0, held // block)
            def _(r):
                rows_of(pl.ds(pl.multiple_of(r * block, block), block))

        for i in range(outs):
            out_refs[i][...] = y_ref[i * back : (i + 1) * back, :]

    return list(
        pl.pallas_call(
            body,
            out_shape=out,
            in_specs=[whole(x) for x in ins] + [whole(w) for w in weights] + unread(after),
            out_specs=[whole(o) for o in out],
            scratch_shapes=[VMEM((held, width), jnp.bfloat16)] * 2,
            compiler_params=params(24),
            cost_estimate=taking(microseconds),
            name="expert",
        )(*ins, *weights, *after)
    )


def relay_back(returned, rows_in, top, cap, after, microseconds):
    half = len(returned)
    rows, width = rows_in.shape[0], returned[0].shape[1]
    out = jax.ShapeDtypeStruct((rows, width), jnp.bfloat16)

    def body(rows_ref, *refs):
        in_refs, (out_ref, joined) = refs[:half], refs[half + len(after) :]
        for d in range(half):
            joined[d * cap : (d + 1) * cap, :] = in_refs[d][...]
        far = weighted_rows(unpack_route(rows_ref[:, width:], top), half, joined, cap)
        out_ref[...] = far.astype(jnp.bfloat16)

    return pl.pallas_call(
        body,
        out_shape=out,
        in_specs=[whole(rows_in)] + [whole(returned[0])] * half + unread(after),
        out_specs=whole(out),
        scratch_shapes=[VMEM((half * cap, width), jnp.bfloat16)],
        compiler_params=params(24),
        cost_estimate=taking(microseconds),
        name="relay_back",
    )(rows_in, *returned, *after)


def add_near(resid, far, returned, info, cap, after, microseconds):
    half = len(returned)
    chunks = len(resid)
    rows, width = resid[0].shape
    out = jax.ShapeDtypeStruct((rows * chunks, width), jnp.float32)

    def body(info_ref, *refs):
        resid_refs, far_refs, refs = refs[:chunks], refs[chunks : chunks + len(far)], refs[chunks + len(far) :]
        in_refs, (out_ref, joined) = refs[:half], refs[half + len(after) :]
        for c in range(chunks):
            for d in range(half):
                joined[d * cap : (d + 1) * cap, :] = in_refs[d][c * cap : (c + 1) * cap, :]
            total = resid_refs[c][...] + weighted_rows(info_ref[:, c * rows : (c + 1) * rows], half, joined, cap)
            if c < len(far):
                total = total + far_refs[c][...].astype(jnp.float32)
            out_ref[c * rows : (c + 1) * rows, :] = total

    return pl.pallas_call(
        body,
        out_shape=out,
        in_specs=[whole(x) for x in (info, *resid, *far, *returned)] + unread(after),
        out_specs=whole(out),
        scratch_shapes=[VMEM((half * cap, width), jnp.bfloat16)],
        compiler_params=params(24),
        cost_estimate=taking(microseconds),
        name="add_near",
    )(info, *resid, *far, *returned, *after)


def add_far(base, far):
    total, width = base.shape
    first = total - far.shape[0]
    out = jax.ShapeDtypeStruct(base.shape, jnp.bfloat16)

    def body(base_ref, far_ref, out_ref):
        if first:
            out_ref[:first, :] = base_ref[:first, :].astype(jnp.bfloat16)
        out_ref[first:, :] = (base_ref[first:, :] + far_ref[...].astype(jnp.float32)).astype(jnp.bfloat16)

    return pl.pallas_call(
        body,
        out_shape=out,
        in_specs=[whole(base), whole(far)],
        out_specs=whole(out),
        compiler_params=params(24),
        cost_estimate=taking(1),
        name="add_far",
    )(base, far)


def around(parts):
    moved = {d: exchange(parts[d], 2 * d) for d in reversed(range(1, len(parts)))}
    return [parts[0]] + [moved[d] for d in range(1, len(parts))]


def local(
    hidden_in,
    queries,
    token_keys,
    token_values,
    stored_keys,
    stored_values,
    cache_len,
    query_gain,
    k_gain,
    norm_gain,
    expert_ids,
    gate_weights,
    w_gate,
    w_up,
    w_down,
):
    token_rows, top = expert_ids.shape
    ep = lax.axis_size("ep")
    experts = ep // 2
    half = experts // 2
    slots = 2 * token_rows * top // experts
    chunks = 2 if slots >= 32 else 1
    cap = slots // chunks
    rows = token_rows // chunks
    arrays = (
        queries,
        hidden_in,
        stored_keys,
        stored_values,
        token_keys,
        token_values,
        query_gain,
        k_gain,
        norm_gain,
        expert_ids.T,
        gate_weights.T,
    )
    arrays = tuple(pltpu.with_memory_space_constraint(x, pltpu.HBM) for x in arrays)
    weights = (w_gate, w_up, w_down)
    weights = weights + tuple(exchange(w, 1) for w in weights)

    resid, normed, outgoing, info = [], [], [], None
    for c in range(chunks):
        residual, rows_c, outgoing, packed = attend(cache_len, arrays, outgoing, c, chunks, half, cap)
        info = packed if c == 0 else info
        resid.append(residual)
        normed.append(rows_c)
    far_rows = [exchange(normed[0], ep // 2)]
    gate = passed(outgoing, list(weights[3:]), 0.3)
    near = around(gate)
    after = gate[:1]
    for c in range(1, chunks):
        after = passed([normed[c]], after, 0.3)
        far_rows.append(exchange(after[0], ep // 2))

    placed = []
    for c in range(chunks):
        slotted, _ = relay(far_rows[c], top, half, cap, [], after, 0.5)
        placed.append(around(slotted))
        after = [slotted[0], *near]
    returned, after = [], after[:1]
    for c in range(chunks):
        outs = expert(placed[c], weights, half, after, 0.01)
        returned.append(around(outs))
        after = outs[:1]
    far_back, near_back = [], [None] * half
    for c in range(chunks):
        if c == chunks - 1:
            near_out = expert(near, weights, half, after, 4)
            near_back[0] = near_out[0]
            after = passed(near_out[half - 1 :], near_out[:1], 0.1)
            near_back[half - 1] = exchange(after[0], 2 * (half - 1))
        back = relay_back(returned[c], far_rows[c], top, cap, after, 0.6)
        far_back.append(exchange(back, ep // 2))
        after = [back]
    rest = passed(near_out[1 : half - 1], after, 0.1)
    for d in range(1, half - 1):
        near_back[d] = exchange(rest[d - 1], 2 * d)
    base = add_near(resid, far_back[:-1], near_back, info, cap, rest[:1], 4)
    return add_far(base, far_back[-1])


def solution(mesh):
    in_specs = (
        P(("grp", "ep"), None),
        P(("grp", "ep"), None),
        P(("grp", "ep"), None),
        P(("grp", "ep"), None),
        P(("grp", "ep"), None),
        P(("grp", "ep"), None),
        P(("grp", "ep")),
        P(),
        P(),
        P(),
        P(("grp", "ep"), None),
        P(("grp", "ep"), None),
        P(None, "ep"),
        P(None, "ep"),
        P("ep", None),
    )
    out_specs = P(("grp", "ep"), None)
    return jax.shard_map(local, mesh=mesh, in_specs=in_specs, out_specs=out_specs, check_vma=False)
```

```python
import math

import jax
import jax.numpy as jnp
from jax import lax
from jax.experimental import pallas as pl
from jax.experimental.pallas import tpu as pltpu
from jax.sharding import PartitionSpec as P

EPS = 1e-06
ROUTE = 128
MIB = 1 << 20
VMEM = pltpu.VMEM
SMEM = pltpu.SMEM


def exchange(value, distance):
    return lax.ppermute(value, "ep", [(i, i ^ distance) for i in range(lax.axis_size("ep"))])


def whole(array):
    return pl.BlockSpec(array.shape, lambda: (0,) * array.ndim, memory_space=VMEM)


def params(mib):
    return pltpu.CompilerParams(vmem_limit_bytes=mib * MIB)


def unread(arrays):
    return [pl.BlockSpec(memory_space=pl.ANY)] * len(arrays)


def taking(microseconds):
    return pl.CostEstimate(flops=1, bytes_accessed=int(microseconds * 3.5e6), transcendentals=0)


def slots_of(half, cap):
    chip = lax.axis_index("ep") // 2
    lane = lax.broadcasted_iota(jnp.int32, (half * cap, 1), 0)
    apart = lane // cap
    position = chip & (half - 1)
    expert = (chip - position) + (apart ^ position)
    return expert.astype(jnp.float32), (lane - apart * cap).astype(jnp.float32)


def slot_hits(info, expert, slot):
    width, rows = info.shape
    named = info[0:1, :] == expert
    for k in range(1, width // 2):
        named = jnp.logical_or(named, info[k : k + 1, :] == expert)
    row = lax.broadcasted_iota(jnp.int32, (rows, rows), 0)
    col = lax.broadcasted_iota(jnp.int32, (rows, rows), 1)
    earlier = jnp.where(row < col, 1.0, 0.0).astype(jnp.bfloat16)
    ones = jnp.where(named, 1.0, 0.0)
    rank = jnp.dot(ones.astype(jnp.bfloat16), earlier, preferred_element_type=jnp.float32)
    return jnp.where(rank == slot, ones, 0.0)


def route_lanes(top, width):
    row = lax.broadcasted_iota(jnp.int32, (2 * top, width), 0)
    lane = lax.broadcasted_iota(jnp.int32, (2 * top, width), 1)
    apart = lane - row
    gate = row >= top
    later = jnp.logical_and(gate, jnp.logical_or(apart == top, apart == 2 * top))
    return jnp.where(jnp.logical_or(apart == 0, later), 1.0, 0.0).astype(jnp.bfloat16)


def pack_route(info, width):
    top = info.shape[0] // 2
    gates = info[top:, :]
    high = gates.astype(jnp.bfloat16).astype(jnp.float32)
    middle = (gates - high).astype(jnp.bfloat16).astype(jnp.float32)
    low = gates - high - middle
    parts = jnp.concatenate([info[:top, :], high, middle, low], axis=0).astype(jnp.bfloat16)
    row = lax.broadcasted_iota(jnp.int32, (4 * top, width), 0)
    lane = lax.broadcasted_iota(jnp.int32, (4 * top, width), 1)
    place = jnp.where(row == lane, 1.0, 0.0).astype(jnp.bfloat16)
    return lax.dot_general(parts, place, (((0,), (0,)), ((), ())), preferred_element_type=jnp.float32).astype(
        jnp.bfloat16
    )


def unpack_route(lanes, top):
    return lax.dot_general(
        route_lanes(top, lanes.shape[1]), lanes, (((1,), (1,)), ((), ())), preferred_element_type=jnp.float32
    )


def spread_rows(info, rows_bf16, out_refs, cap):
    half = len(out_refs)
    expert, slot = slots_of(half, cap)
    hits = slot_hits(info, expert, slot).astype(jnp.bfloat16)
    placed = jnp.dot(hits, rows_bf16, preferred_element_type=jnp.float32).astype(jnp.bfloat16)
    for d in range(half):
        out_refs[d][...] = placed[d * cap : (d + 1) * cap, :]


def weighted_rows(info, half, joined, cap):
    top = info.shape[0] // 2
    expert, slot = slots_of(half, cap)
    hits = slot_hits(info, expert, slot)
    weight = jnp.zeros_like(hits)
    for k in range(top):
        weight = weight + jnp.where(info[k : k + 1, :] == expert, info[top + k : top + k + 1, :], 0.0)
    weight = weight * hits
    high = weight.astype(jnp.bfloat16)
    low = (weight - high.astype(jnp.float32)).astype(jnp.bfloat16)
    values = joined[...]
    first = (((0,), (0,)), ((), ()))
    return lax.dot_general(high, values, first, preferred_element_type=jnp.float32) + lax.dot_general(
        low, values, first, preferred_element_type=jnp.float32
    )


def unit_rows(values, gain, ones):
    square = jnp.dot((values * values).astype(jnp.bfloat16), ones, preferred_element_type=jnp.float32)
    return values * lax.rsqrt(square / values.shape[-1] + EPS) * gain


def attend(cache_len, arrays, before, chunk, chunks, half, cap):
    queries, hidden_in, stored_keys, stored_values, token_keys, token_values = arrays[:6]
    ids, gates = arrays[9:]
    rows, width = hidden_in.shape[0] // chunks, hidden_in.shape[1]
    cache_rows, kv_width = stored_keys.shape
    token_rows = token_keys.shape[0]
    head = arrays[6].shape[0]
    heads_kv = kv_width // head
    heads = width // head
    group = heads // heads_kv
    keys = cache_rows + token_rows
    top = ids.shape[0]
    first, last = chunk == 0, chunk == chunks - 1
    mine = pl.ds(chunk * rows, rows)
    per = max(1, min(group, 256 // rows))
    block = per * rows
    out_shape = [
        jax.ShapeDtypeStruct((rows, width), jnp.float32),
        jax.ShapeDtypeStruct((rows, width + ROUTE), jnp.bfloat16),
    ]
    if last:
        out_shape += [jax.ShapeDtypeStruct((cap * chunks, width), jnp.bfloat16)] * half
    if first:
        out_shape.append(jax.ShapeDtypeStruct((2 * top, token_rows), jnp.float32))

    def body(len_hbm, *refs):
        hbm, refs = refs[:11], refs[11:]
        carried, refs = refs[: len(before)], refs[len(before) :]
        outs, scratch = refs[: len(out_shape)], refs[len(out_shape) :]
        (q_ref, hid_ref, sk_ref, sv_ref, tk_ref, tv_ref, qg_ref, kg_ref, ng_ref, ids_ref, gates_ref) = scratch[:11]
        kn_ref, vx_ref, qs_ref, info_ref, len_ref, sems = scratch[11:]
        resid_ref, normed_ref, out_refs = outs[0], outs[1], outs[2 : 2 + half] if last else []
        copies = []
        for i in range(11):
            source = hbm[i].at[mine, :] if i < 2 else hbm[i]
            target = scratch[i].at[0] if 6 <= i < 9 else scratch[i]
            copies.append(pltpu.make_async_copy(source, target, sems.at[i]))
        copies.append(pltpu.make_async_copy(len_hbm, len_ref, sems.at[11]))
        for i in (0, 6, 11, 2, 7, 4, 3, 5, 9, 10, 1, 8):
            copies[i].start()
        ones = jnp.ones((head, head), jnp.bfloat16)
        for i in (0, 6):
            copies[i].wait()
        q_gain = qg_ref[...] * (math.log2(math.e) / math.sqrt(head))
        for h in range(heads):
            x = q_ref[:, h * head : (h + 1) * head].astype(jnp.float32)
            qs_ref[h * rows : (h + 1) * rows, :] = unit_rows(x, q_gain, ones).astype(jnp.bfloat16)
        for i in (2, 7, 4):
            copies[i].wait()
        k_gain = kg_ref[...]
        for g in range(heads_kv):
            cols = slice(g * head, (g + 1) * head)
            kn_ref[g, :cache_rows, :] = unit_rows(sk_ref[:, cols].astype(jnp.float32), k_gain, ones).astype(
                jnp.bfloat16
            )
            kn_ref[g, cache_rows:, :] = unit_rows(tk_ref[:, cols].astype(jnp.float32), k_gain, ones).astype(
                jnp.bfloat16
            )
        for i in (11, 3, 5):
            copies[i].wait()
        live = lax.broadcasted_iota(jnp.int32, (cache_rows, head), 0) < len_ref[0]
        live_ones = jnp.where(live, 1.0, 0.0).astype(jnp.bfloat16)
        for g in range(heads_kv):
            cols = slice(g * head, (g + 1) * head)
            vx_ref[g, :cache_rows, :head] = sv_ref[:, cols] * live_ones
            vx_ref[g, :cache_rows, head:] = live_ones
            vx_ref[g, cache_rows:, :head] = tv_ref[:, cols]
            vx_ref[g, cache_rows:, head:] = jnp.ones((token_rows, head), jnp.bfloat16)
        for i in (9, 10, 1, 8):
            copies[i].wait()
        info_ref[:top, :] = ids_ref[...].astype(jnp.float32)
        info_ref[top:, :] = gates_ref[...]
        if first:
            outs[-1][...] = info_ref[...]
        own = lax.broadcasted_iota(jnp.int32, (block, token_rows), 0) % rows + chunk * rows
        causal = lax.broadcasted_iota(jnp.int32, (block, token_rows), 1) <= own
        square = jnp.zeros((rows, head), jnp.float32)
        last_dims = (((1,), (1,)), ((), ()))
        for b in range(heads // per):
            g = b * per // group
            q_block = qs_ref[b * block : (b + 1) * block, :]
            scores = lax.dot_general(q_block, kn_ref[g, :cache_rows, :], last_dims, preferred_element_type=jnp.float32)
            raised = jnp.exp2(scores).astype(jnp.bfloat16)
            scores_new = lax.dot_general(
                q_block, kn_ref[g, cache_rows:, :], last_dims, preferred_element_type=jnp.float32
            )
            raised_new = jnp.where(causal, jnp.exp2(scores_new), 0.0).astype(jnp.bfloat16)
            summed = jnp.dot(raised, vx_ref[g, :cache_rows, :], preferred_element_type=jnp.float32) + jnp.dot(
                raised_new, vx_ref[g, cache_rows:, :], preferred_element_type=jnp.float32
            )
            attended = (summed[:, :head] / summed[:, head:]).astype(jnp.bfloat16).astype(jnp.float32)
            for i in range(per):
                cols = slice((b * per + i) * head, (b * per + i + 1) * head)
                resid = hid_ref[:, cols].astype(jnp.float32) + attended[i * rows : (i + 1) * rows, :]
                resid_ref[:, cols] = resid
                square = square + resid * resid
        scale = lax.rsqrt(jnp.sum(square, axis=-1, keepdims=True) / width + EPS)
        normed = (resid_ref[...] * scale * ng_ref[...]).astype(jnp.bfloat16)
        route = info_ref[:, chunk * rows : (chunk + 1) * rows]
        normed_ref[:, :width] = normed
        normed_ref[:, width:] = pack_route(route, ROUTE)
        if last:
            for c in range(chunks):
                spread_rows(
                    info_ref[:, c * rows : (c + 1) * rows],
                    carried[c][:, :width] if c < len(carried) else normed,
                    [o.at[c * cap : (c + 1) * cap, :] for o in out_refs],
                    cap,
                )

    results = pl.pallas_call(
        body,
        out_shape=out_shape,
        in_specs=[pl.BlockSpec(memory_space=pl.ANY)]
        + [pl.BlockSpec(memory_space=pltpu.HBM)] * 11
        + [whole(b) for b in before],
        out_specs=[whole(o) for o in out_shape],
        scratch_shapes=[
            VMEM((rows, width), jnp.bfloat16),
            VMEM((rows, width), jnp.bfloat16),
            VMEM((cache_rows, kv_width), jnp.bfloat16),
            VMEM((cache_rows, kv_width), jnp.bfloat16),
            VMEM((token_rows, kv_width), jnp.bfloat16),
            VMEM((token_rows, kv_width), jnp.bfloat16),
            VMEM((1, head), jnp.float32),
            VMEM((1, head), jnp.float32),
            VMEM((1, width), jnp.float32),
            VMEM((top, token_rows), jnp.int32),
            VMEM((top, token_rows), jnp.float32),
            VMEM((heads_kv, keys, head), jnp.bfloat16),
            VMEM((heads_kv, keys, 2 * head), jnp.bfloat16),
            VMEM((rows * heads, head), jnp.bfloat16),
            VMEM((2 * top, token_rows), jnp.float32),
            SMEM((1,), jnp.int32),
            pltpu.SemaphoreType.DMA((12,)),
        ],
        compiler_params=params(24),
        cost_estimate=taking(4),
        name="attend",
    )(cache_len, *arrays, *before)
    return results[0], results[1], list(results[2 : 2 + half]) if last else [], (results[-1] if first else None)


def relay(rows_in, top, half, cap, carried, after, microseconds):
    width = rows_in.shape[1] - ROUTE
    out = [jax.ShapeDtypeStruct((cap, width), jnp.bfloat16)] * half
    out += [jax.ShapeDtypeStruct(x.shape, x.dtype) for x in carried]

    def body(rows_ref, *refs):
        outs = refs[len(carried) + len(after) :]
        spread_rows(unpack_route(rows_ref[:, width:], top), rows_ref[:, :width], outs[:half], cap)
        for i in range(len(carried)):
            outs[half + i][...] = refs[i][...]

    results = pl.pallas_call(
        body,
        out_shape=out,
        in_specs=[whole(rows_in)] + [whole(x) for x in carried] + unread(after),
        out_specs=[whole(o) for o in out],
        compiler_params=params(24),
        cost_estimate=taking(microseconds),
        name="relay",
    )(rows_in, *carried, *after)
    return list(results[:half]), list(results[half:])


def passed(arrays, after, microseconds):
    def body(*refs):
        outs = refs[len(arrays) + len(after) :]
        for i in range(len(arrays)):
            outs[i][...] = refs[i][...]

    return list(
        pl.pallas_call(
            body,
            out_shape=[jax.ShapeDtypeStruct(x.shape, x.dtype) for x in arrays],
            in_specs=[whole(x) for x in arrays] + unread(after),
            out_specs=[whole(x) for x in arrays],
            compiler_params=params(24),
            cost_estimate=taking(microseconds),
            name="passed",
        )(*arrays, *after)
    )


def expert(ins, weights, outs, after, microseconds):
    rows, width = ins[0].shape
    total = len(ins) * rows
    hidden = weights[0].shape[1]
    block = 128
    held = -(-total // block) * block
    part = 1024
    back = total // outs
    out = [jax.ShapeDtypeStruct((back, width), jnp.bfloat16)] * outs

    def body(*refs):
        in_refs, refs = refs[: len(ins)], refs[len(ins) :]
        (wg0, wu0, wd0, wg1, wu1, wd1), refs = refs[:6], refs[6 + len(after) :]
        out_refs, (x_ref, y_ref) = refs[:outs], refs[outs:]
        for i in range(len(ins)):
            x_ref[i * rows : (i + 1) * rows, :] = in_refs[i][...]

        if held > total:
            x_ref[total:, :] = jnp.zeros((held - total, width), jnp.bfloat16)

        def rows_of(span):
            inners = []
            for wg, wu in ((wg0, wu0), (wg1, wu1)):
                both = jnp.concatenate([wg[...], wu[...]], axis=1)
                pre = jnp.dot(x_ref[span, :], both, preferred_element_type=jnp.float32)
                gate = pre[:, :hidden]
                inners.append((gate / (1.0 + jnp.exp(-gate)) * pre[:, hidden:]).astype(jnp.bfloat16))
            inner = jnp.concatenate(inners, axis=1)
            for k in range(0, width, part):
                down = jnp.concatenate([wd0[:, k : k + part], wd1[:, k : k + part]], axis=0)
                y_ref[span, k : k + part] = jnp.dot(inner, down, preferred_element_type=jnp.float32).astype(
                    jnp.bfloat16
                )

        if held == block:
            rows_of(slice(0, block))
        else:

            @pl.loop(0, held // block)
            def _(r):
                rows_of(pl.ds(pl.multiple_of(r * block, block), block))

        for i in range(outs):
            out_refs[i][...] = y_ref[i * back : (i + 1) * back, :]

    return list(
        pl.pallas_call(
            body,
            out_shape=out,
            in_specs=[whole(x) for x in ins] + [whole(w) for w in weights] + unread(after),
            out_specs=[whole(o) for o in out],
            scratch_shapes=[VMEM((held, width), jnp.bfloat16)] * 2,
            compiler_params=params(24),
            cost_estimate=taking(microseconds),
            name="expert",
        )(*ins, *weights, *after)
    )


def relay_back(returned, rows_in, top, cap, after, microseconds):
    half = len(returned)
    rows, width = rows_in.shape[0], returned[0].shape[1]
    out = jax.ShapeDtypeStruct((rows, width), jnp.bfloat16)

    def body(rows_ref, *refs):
        in_refs, (out_ref, joined) = refs[:half], refs[half + len(after) :]
        for d in range(half):
            joined[d * cap : (d + 1) * cap, :] = in_refs[d][...]
        far = weighted_rows(unpack_route(rows_ref[:, width:], top), half, joined, cap)
        out_ref[...] = far.astype(jnp.bfloat16)

    return pl.pallas_call(
        body,
        out_shape=out,
        in_specs=[whole(rows_in)] + [whole(returned[0])] * half + unread(after),
        out_specs=whole(out),
        scratch_shapes=[VMEM((half * cap, width), jnp.bfloat16)],
        compiler_params=params(24),
        cost_estimate=taking(microseconds),
        name="relay_back",
    )(rows_in, *returned, *after)


def add_near(resid, far, returned, info, cap, after, microseconds):
    half = len(returned)
    chunks = len(resid)
    rows, width = resid[0].shape
    out = jax.ShapeDtypeStruct((rows * chunks, width), jnp.float32)

    def body(info_ref, *refs):
        resid_refs, far_refs, refs = refs[:chunks], refs[chunks : chunks + len(far)], refs[chunks + len(far) :]
        in_refs, (out_ref, joined) = refs[:half], refs[half + len(after) :]
        for c in range(chunks):
            for d in range(half):
                joined[d * cap : (d + 1) * cap, :] = in_refs[d][c * cap : (c + 1) * cap, :]
            total = resid_refs[c][...] + weighted_rows(info_ref[:, c * rows : (c + 1) * rows], half, joined, cap)
            if c < len(far):
                total = total + far_refs[c][...].astype(jnp.float32)
            out_ref[c * rows : (c + 1) * rows, :] = total

    return pl.pallas_call(
        body,
        out_shape=out,
        in_specs=[whole(x) for x in (info, *resid, *far, *returned)] + unread(after),
        out_specs=whole(out),
        scratch_shapes=[VMEM((half * cap, width), jnp.bfloat16)],
        compiler_params=params(24),
        cost_estimate=taking(microseconds),
        name="add_near",
    )(info, *resid, *far, *returned, *after)


def add_far(base, far):
    total, width = base.shape
    first = total - far.shape[0]
    out = jax.ShapeDtypeStruct(base.shape, jnp.bfloat16)

    def body(base_ref, far_ref, out_ref):
        if first:
            out_ref[:first, :] = base_ref[:first, :].astype(jnp.bfloat16)
        out_ref[first:, :] = (base_ref[first:, :] + far_ref[...].astype(jnp.float32)).astype(jnp.bfloat16)

    return pl.pallas_call(
        body,
        out_shape=out,
        in_specs=[whole(base), whole(far)],
        out_specs=whole(out),
        compiler_params=params(24),
        cost_estimate=taking(1),
        name="add_far",
    )(base, far)


def around(parts):
    moved = {d: exchange(parts[d], 2 * d) for d in reversed(range(1, len(parts)))}
    return [parts[0]] + [moved[d] for d in range(1, len(parts))]


def local(
    hidden_in,
    queries,
    token_keys,
    token_values,
    stored_keys,
    stored_values,
    cache_len,
    query_gain,
    k_gain,
    norm_gain,
    expert_ids,
    gate_weights,
    w_gate,
    w_up,
    w_down,
):
    token_rows, top = expert_ids.shape
    ep = lax.axis_size("ep")
    experts = ep // 2
    half = experts // 2
    slots = 2 * token_rows * top // experts
    chunks = 2 if slots >= 32 else 1
    cap = slots // chunks
    rows = token_rows // chunks
    arrays = (
        queries,
        hidden_in,
        stored_keys,
        stored_values,
        token_keys,
        token_values,
        query_gain,
        k_gain,
        norm_gain,
        expert_ids.T,
        gate_weights.T,
    )
    arrays = tuple(pltpu.with_memory_space_constraint(x, pltpu.HBM) for x in arrays)
    weights = (w_gate, w_up, w_down)
    weights = weights + tuple(exchange(w, 1) for w in weights)

    resid, normed, outgoing, info = [], [], [], None
    for c in range(chunks):
        residual, rows_c, outgoing, packed = attend(cache_len, arrays, normed, c, chunks, half, cap)
        info = packed if c == 0 else info
        resid.append(residual)
        normed.append(rows_c)
    far_rows = [exchange(normed[0], ep // 2)]
    gate = passed(outgoing, list(weights[3:]), 0.3)
    near = around(gate)
    after = gate[:1]
    for c in range(1, chunks):
        after = passed([normed[c]], after, 0.3)
        far_rows.append(exchange(after[0], ep // 2))

    placed = []
    for c in range(chunks):
        slotted, _ = relay(far_rows[c], top, half, cap, [], after, 0.5)
        placed.append(around(slotted))
        after = [slotted[0], *near]
    returned, after = [], after[:1]
    for c in range(chunks):
        outs = expert(placed[c], weights, half, after, 0.01)
        returned.append(around(outs))
        after = outs[:1]
    far_back, near_back = [], [None] * half
    for c in range(chunks):
        if c == chunks - 1:
            near_out = expert(near, weights, half, after, 4)
            near_back[0] = near_out[0]
            after = passed(near_out[half - 1 :], near_out[:1], 0.1)
            near_back[half - 1] = exchange(after[0], 2 * (half - 1))
        back = relay_back(returned[c], far_rows[c], top, cap, after, 0.6)
        far_back.append(exchange(back, ep // 2))
        after = [back]
    rest = passed(near_out[1 : half - 1], after, 0.1)
    for d in range(1, half - 1):
        near_back[d] = exchange(rest[d - 1], 2 * d)
    base = add_near(resid, far_back[:-1], near_back, info, cap, rest[:1], 4)
    return add_far(base, far_back[-1])


def solution(mesh):
    in_specs = (
        P(("grp", "ep"), None),
        P(("grp", "ep"), None),
        P(("grp", "ep"), None),
        P(("grp", "ep"), None),
        P(("grp", "ep"), None),
        P(("grp", "ep"), None),
        P(("grp", "ep")),
        P(),
        P(),
        P(),
        P(("grp", "ep"), None),
        P(("grp", "ep"), None),
        P(None, "ep"),
        P(None, "ep"),
        P("ep", None),
    )
    out_specs = P(("grp", "ep"), None)
    return jax.shard_map(local, mesh=mesh, in_specs=in_specs, out_specs=out_specs, check_vma=False)
```

```python
import math

import jax
import jax.numpy as jnp
from jax import lax
from jax.experimental import pallas as pl
from jax.experimental.pallas import tpu as pltpu
from jax.sharding import PartitionSpec as P

EPS = 1e-06
ROUTE = 128
MIB = 1 << 20
VMEM = pltpu.VMEM
SMEM = pltpu.SMEM


def exchange(value, distance):
    return lax.ppermute(value, "ep", [(i, i ^ distance) for i in range(lax.axis_size("ep"))])


def whole(array):
    return pl.BlockSpec(array.shape, lambda: (0,) * array.ndim, memory_space=VMEM)


def params(mib):
    return pltpu.CompilerParams(vmem_limit_bytes=mib * MIB)


def unread(arrays):
    return [pl.BlockSpec(memory_space=pl.ANY)] * len(arrays)


def taking(microseconds):
    return pl.CostEstimate(flops=1, bytes_accessed=int(microseconds * 3.5e6), transcendentals=0)


def slots_of(half, cap):
    chip = lax.axis_index("ep") // 2
    lane = lax.broadcasted_iota(jnp.int32, (half * cap, 1), 0)
    apart = lane // cap
    position = chip & (half - 1)
    expert = (chip - position) + (apart ^ position)
    return expert.astype(jnp.float32), (lane - apart * cap).astype(jnp.float32)


def slot_hits(info, expert, slot):
    width, rows = info.shape
    named = info[0:1, :] == expert
    for k in range(1, width // 2):
        named = jnp.logical_or(named, info[k : k + 1, :] == expert)
    row = lax.broadcasted_iota(jnp.int32, (rows, rows), 0)
    col = lax.broadcasted_iota(jnp.int32, (rows, rows), 1)
    earlier = jnp.where(row < col, 1.0, 0.0).astype(jnp.bfloat16)
    ones = jnp.where(named, 1.0, 0.0)
    rank = jnp.dot(ones.astype(jnp.bfloat16), earlier, preferred_element_type=jnp.float32)
    return jnp.where(rank == slot, ones, 0.0)


def route_lanes(top, width):
    row = lax.broadcasted_iota(jnp.int32, (2 * top, width), 0)
    lane = lax.broadcasted_iota(jnp.int32, (2 * top, width), 1)
    apart = lane - row
    gate = row >= top
    later = jnp.logical_and(gate, jnp.logical_or(apart == top, apart == 2 * top))
    return jnp.where(jnp.logical_or(apart == 0, later), 1.0, 0.0).astype(jnp.bfloat16)


def pack_route(info, width):
    top = info.shape[0] // 2
    gates = info[top:, :]
    high = gates.astype(jnp.bfloat16).astype(jnp.float32)
    middle = (gates - high).astype(jnp.bfloat16).astype(jnp.float32)
    low = gates - high - middle
    parts = jnp.concatenate([info[:top, :], high, middle, low], axis=0).astype(jnp.bfloat16)
    row = lax.broadcasted_iota(jnp.int32, (4 * top, width), 0)
    lane = lax.broadcasted_iota(jnp.int32, (4 * top, width), 1)
    place = jnp.where(row == lane, 1.0, 0.0).astype(jnp.bfloat16)
    return lax.dot_general(parts, place, (((0,), (0,)), ((), ())), preferred_element_type=jnp.float32).astype(
        jnp.bfloat16
    )


def unpack_route(lanes, top):
    return lax.dot_general(
        route_lanes(top, lanes.shape[1]), lanes, (((1,), (1,)), ((), ())), preferred_element_type=jnp.float32
    )


def spread_rows(info, rows_bf16, out_refs, cap):
    half = len(out_refs)
    expert, slot = slots_of(half, cap)
    hits = slot_hits(info, expert, slot).astype(jnp.bfloat16)
    placed = jnp.dot(hits, rows_bf16, preferred_element_type=jnp.float32).astype(jnp.bfloat16)
    for d in range(half):
        out_refs[d][...] = placed[d * cap : (d + 1) * cap, :]


def weighted_rows(info, half, joined, cap):
    top = info.shape[0] // 2
    expert, slot = slots_of(half, cap)
    hits = slot_hits(info, expert, slot)
    weight = jnp.zeros_like(hits)
    for k in range(top):
        weight = weight + jnp.where(info[k : k + 1, :] == expert, info[top + k : top + k + 1, :], 0.0)
    weight = weight * hits
    high = weight.astype(jnp.bfloat16)
    low = (weight - high.astype(jnp.float32)).astype(jnp.bfloat16)
    values = joined[...]
    first = (((0,), (0,)), ((), ()))
    both = jnp.concatenate([high, low], axis=0)
    twice = jnp.concatenate([values, values], axis=0)
    return lax.dot_general(both, twice, first, preferred_element_type=jnp.float32)


def unit_rows(values, gain, ones):
    square = jnp.dot((values * values).astype(jnp.bfloat16), ones, preferred_element_type=jnp.float32)
    return values * lax.rsqrt(square / values.shape[-1] + EPS) * gain


def attend(cache_len, arrays, before, chunk, chunks, half, cap):
    queries, hidden_in, stored_keys, stored_values, token_keys, token_values = arrays[:6]
    ids, gates = arrays[9:]
    rows, width = hidden_in.shape[0] // chunks, hidden_in.shape[1]
    cache_rows, kv_width = stored_keys.shape
    token_rows = token_keys.shape[0]
    head = arrays[6].shape[0]
    heads_kv = kv_width // head
    heads = width // head
    group = heads // heads_kv
    keys = cache_rows + token_rows
    top = ids.shape[0]
    first, last = chunk == 0, chunk == chunks - 1
    mine = pl.ds(chunk * rows, rows)
    per = max(1, min(group, 256 // rows))
    block = per * rows
    out_shape = [
        jax.ShapeDtypeStruct((rows, width), jnp.float32),
        jax.ShapeDtypeStruct((rows, width + ROUTE), jnp.bfloat16),
    ]
    if last:
        out_shape += [jax.ShapeDtypeStruct((cap * chunks, width), jnp.bfloat16)] * half
    if first:
        out_shape.append(jax.ShapeDtypeStruct((2 * top, token_rows), jnp.float32))

    def body(len_hbm, *refs):
        hbm, refs = refs[:11], refs[11:]
        carried, refs = refs[: len(before)], refs[len(before) :]
        outs, scratch = refs[: len(out_shape)], refs[len(out_shape) :]
        (q_ref, hid_ref, sk_ref, sv_ref, tk_ref, tv_ref, qg_ref, kg_ref, ng_ref, ids_ref, gates_ref) = scratch[:11]
        kn_ref, vx_ref, qs_ref, info_ref, len_ref, sems = scratch[11:]
        resid_ref, normed_ref, out_refs = outs[0], outs[1], outs[2 : 2 + half] if last else []
        copies = []
        for i in range(11):
            source = hbm[i].at[mine, :] if i < 2 else hbm[i]
            target = scratch[i].at[0] if 6 <= i < 9 else scratch[i]
            copies.append(pltpu.make_async_copy(source, target, sems.at[i]))
        copies.append(pltpu.make_async_copy(len_hbm, len_ref, sems.at[11]))
        for i in (0, 6, 11, 2, 7, 4, 3, 5, 9, 10, 1, 8):
            copies[i].start()
        ones = jnp.ones((head, head), jnp.bfloat16)
        for i in (0, 6):
            copies[i].wait()
        q_gain = qg_ref[...] * (math.log2(math.e) / math.sqrt(head))
        for h in range(heads):
            x = q_ref[:, h * head : (h + 1) * head].astype(jnp.float32)
            qs_ref[h * rows : (h + 1) * rows, :] = unit_rows(x, q_gain, ones).astype(jnp.bfloat16)
        for i in (2, 7, 4):
            copies[i].wait()
        k_gain = kg_ref[...]
        for g in range(heads_kv):
            cols = slice(g * head, (g + 1) * head)
            kn_ref[g, :cache_rows, :] = unit_rows(sk_ref[:, cols].astype(jnp.float32), k_gain, ones).astype(
                jnp.bfloat16
            )
            kn_ref[g, cache_rows:, :] = unit_rows(tk_ref[:, cols].astype(jnp.float32), k_gain, ones).astype(
                jnp.bfloat16
            )
        for i in (11, 3, 5):
            copies[i].wait()
        live = lax.broadcasted_iota(jnp.int32, (cache_rows, head), 0) < len_ref[0]
        live_ones = jnp.where(live, 1.0, 0.0).astype(jnp.bfloat16)
        for g in range(heads_kv):
            cols = slice(g * head, (g + 1) * head)
            vx_ref[g, :cache_rows, :head] = sv_ref[:, cols] * live_ones
            vx_ref[g, :cache_rows, head:] = live_ones
            vx_ref[g, cache_rows:, :head] = tv_ref[:, cols]
            vx_ref[g, cache_rows:, head:] = jnp.ones((token_rows, head), jnp.bfloat16)
        for i in (9, 10, 1, 8):
            copies[i].wait()
        info_ref[:top, :] = ids_ref[...].astype(jnp.float32)
        info_ref[top:, :] = gates_ref[...]
        if first:
            outs[-1][...] = info_ref[...]
        own = lax.broadcasted_iota(jnp.int32, (block, token_rows), 0) % rows + chunk * rows
        causal = lax.broadcasted_iota(jnp.int32, (block, token_rows), 1) <= own
        square = jnp.zeros((rows, head), jnp.float32)
        last_dims = (((1,), (1,)), ((), ()))
        for b in range(heads // per):
            g = b * per // group
            q_block = qs_ref[b * block : (b + 1) * block, :]
            scores = lax.dot_general(q_block, kn_ref[g, :cache_rows, :], last_dims, preferred_element_type=jnp.float32)
            raised = jnp.exp2(scores).astype(jnp.bfloat16)
            scores_new = lax.dot_general(
                q_block, kn_ref[g, cache_rows:, :], last_dims, preferred_element_type=jnp.float32
            )
            raised_new = jnp.where(causal, jnp.exp2(scores_new), 0.0).astype(jnp.bfloat16)
            summed = jnp.dot(raised, vx_ref[g, :cache_rows, :], preferred_element_type=jnp.float32) + jnp.dot(
                raised_new, vx_ref[g, cache_rows:, :], preferred_element_type=jnp.float32
            )
            attended = (summed[:, :head] / summed[:, head:]).astype(jnp.bfloat16).astype(jnp.float32)
            for i in range(per):
                cols = slice((b * per + i) * head, (b * per + i + 1) * head)
                resid = hid_ref[:, cols].astype(jnp.float32) + attended[i * rows : (i + 1) * rows, :]
                resid_ref[:, cols] = resid
                square = square + resid * resid
        scale = lax.rsqrt(jnp.sum(square, axis=-1, keepdims=True) / width + EPS)
        normed = (resid_ref[...] * scale * ng_ref[...]).astype(jnp.bfloat16)
        route = info_ref[:, chunk * rows : (chunk + 1) * rows]
        normed_ref[:, :width] = normed
        normed_ref[:, width:] = pack_route(route, ROUTE)
        if last:
            for c in range(chunks):
                spread_rows(
                    info_ref[:, c * rows : (c + 1) * rows],
                    carried[c][:, :width] if c < len(carried) else normed,
                    [o.at[c * cap : (c + 1) * cap, :] for o in out_refs],
                    cap,
                )

    results = pl.pallas_call(
        body,
        out_shape=out_shape,
        in_specs=[pl.BlockSpec(memory_space=pl.ANY)]
        + [pl.BlockSpec(memory_space=pltpu.HBM)] * 11
        + [whole(b) for b in before],
        out_specs=[whole(o) for o in out_shape],
        scratch_shapes=[
            VMEM((rows, width), jnp.bfloat16),
            VMEM((rows, width), jnp.bfloat16),
            VMEM((cache_rows, kv_width), jnp.bfloat16),
            VMEM((cache_rows, kv_width), jnp.bfloat16),
            VMEM((token_rows, kv_width), jnp.bfloat16),
            VMEM((token_rows, kv_width), jnp.bfloat16),
            VMEM((1, head), jnp.float32),
            VMEM((1, head), jnp.float32),
            VMEM((1, width), jnp.float32),
            VMEM((top, token_rows), jnp.int32),
            VMEM((top, token_rows), jnp.float32),
            VMEM((heads_kv, keys, head), jnp.bfloat16),
            VMEM((heads_kv, keys, 2 * head), jnp.bfloat16),
            VMEM((rows * heads, head), jnp.bfloat16),
            VMEM((2 * top, token_rows), jnp.float32),
            SMEM((1,), jnp.int32),
            pltpu.SemaphoreType.DMA((12,)),
        ],
        compiler_params=params(24),
        cost_estimate=taking(4),
        name="attend",
    )(cache_len, *arrays, *before)
    return results[0], results[1], list(results[2 : 2 + half]) if last else [], (results[-1] if first else None)


def relay(rows_in, top, half, cap, carried, after, microseconds):
    width = rows_in.shape[1] - ROUTE
    out = [jax.ShapeDtypeStruct((cap, width), jnp.bfloat16)] * half
    out += [jax.ShapeDtypeStruct(x.shape, x.dtype) for x in carried]

    def body(rows_ref, *refs):
        outs = refs[len(carried) + len(after) :]
        spread_rows(unpack_route(rows_ref[:, width:], top), rows_ref[:, :width], outs[:half], cap)
        for i in range(len(carried)):
            outs[half + i][...] = refs[i][...]

    results = pl.pallas_call(
        body,
        out_shape=out,
        in_specs=[whole(rows_in)] + [whole(x) for x in carried] + unread(after),
        out_specs=[whole(o) for o in out],
        compiler_params=params(24),
        cost_estimate=taking(microseconds),
        name="relay",
    )(rows_in, *carried, *after)
    return list(results[:half]), list(results[half:])


def passed(arrays, after, microseconds):
    def body(*refs):
        outs = refs[len(arrays) + len(after) :]
        for i in range(len(arrays)):
            outs[i][...] = refs[i][...]

    return list(
        pl.pallas_call(
            body,
            out_shape=[jax.ShapeDtypeStruct(x.shape, x.dtype) for x in arrays],
            in_specs=[whole(x) for x in arrays] + unread(after),
            out_specs=[whole(x) for x in arrays],
            compiler_params=params(24),
            cost_estimate=taking(microseconds),
            name="passed",
        )(*arrays, *after)
    )


def expert(ins, weights, outs, after, microseconds):
    rows, width = ins[0].shape
    total = len(ins) * rows
    hidden = weights[0].shape[1]
    block = 128
    held = -(-total // block) * block
    part = 1024
    back = total // outs
    out = [jax.ShapeDtypeStruct((back, width), jnp.bfloat16)] * outs

    def body(*refs):
        in_refs, refs = refs[: len(ins)], refs[len(ins) :]
        (wg0, wu0, wd0, wg1, wu1, wd1), refs = refs[:6], refs[6 + len(after) :]
        out_refs, (x_ref, y_ref) = refs[:outs], refs[outs:]
        for i in range(len(ins)):
            x_ref[i * rows : (i + 1) * rows, :] = in_refs[i][...]

        if held > total:
            x_ref[total:, :] = jnp.zeros((held - total, width), jnp.bfloat16)

        def rows_of(span):
            inners = []
            for wg, wu in ((wg0, wu0), (wg1, wu1)):
                both = jnp.concatenate([wg[...], wu[...]], axis=1)
                pre = jnp.dot(x_ref[span, :], both, preferred_element_type=jnp.float32)
                gate = pre[:, :hidden]
                inners.append((gate / (1.0 + jnp.exp(-gate)) * pre[:, hidden:]).astype(jnp.bfloat16))
            inner = jnp.concatenate(inners, axis=1)
            for k in range(0, width, part):
                down = jnp.concatenate([wd0[:, k : k + part], wd1[:, k : k + part]], axis=0)
                y_ref[span, k : k + part] = jnp.dot(inner, down, preferred_element_type=jnp.float32).astype(
                    jnp.bfloat16
                )

        if held == block:
            rows_of(slice(0, block))
        else:

            @pl.loop(0, held // block)
            def _(r):
                rows_of(pl.ds(pl.multiple_of(r * block, block), block))

        for i in range(outs):
            out_refs[i][...] = y_ref[i * back : (i + 1) * back, :]

    return list(
        pl.pallas_call(
            body,
            out_shape=out,
            in_specs=[whole(x) for x in ins] + [whole(w) for w in weights] + unread(after),
            out_specs=[whole(o) for o in out],
            scratch_shapes=[VMEM((held, width), jnp.bfloat16)] * 2,
            compiler_params=params(24),
            cost_estimate=taking(microseconds),
            name="expert",
        )(*ins, *weights, *after)
    )


def relay_back(returned, rows_in, top, cap, after, microseconds):
    half = len(returned)
    rows, width = rows_in.shape[0], returned[0].shape[1]
    out = jax.ShapeDtypeStruct((rows, width), jnp.bfloat16)

    def body(rows_ref, *refs):
        in_refs, (out_ref, joined) = refs[:half], refs[half + len(after) :]
        for d in range(half):
            joined[d * cap : (d + 1) * cap, :] = in_refs[d][...]
        far = weighted_rows(unpack_route(rows_ref[:, width:], top), half, joined, cap)
        out_ref[...] = far.astype(jnp.bfloat16)

    return pl.pallas_call(
        body,
        out_shape=out,
        in_specs=[whole(rows_in)] + [whole(returned[0])] * half + unread(after),
        out_specs=whole(out),
        scratch_shapes=[VMEM((half * cap, width), jnp.bfloat16)],
        compiler_params=params(24),
        cost_estimate=taking(microseconds),
        name="relay_back",
    )(rows_in, *returned, *after)


def add_near(resid, far, returned, info, cap, after, microseconds):
    half = len(returned)
    chunks = len(resid)
    rows, width = resid[0].shape
    out = jax.ShapeDtypeStruct((rows * chunks, width), jnp.float32)

    def body(info_ref, *refs):
        resid_refs, far_refs, refs = refs[:chunks], refs[chunks : chunks + len(far)], refs[chunks + len(far) :]
        in_refs, (out_ref, joined) = refs[:half], refs[half + len(after) :]
        for c in range(chunks):
            for d in range(half):
                joined[d * cap : (d + 1) * cap, :] = in_refs[d][c * cap : (c + 1) * cap, :]
            total = resid_refs[c][...] + weighted_rows(info_ref[:, c * rows : (c + 1) * rows], half, joined, cap)
            if c < len(far):
                total = total + far_refs[c][...].astype(jnp.float32)
            out_ref[c * rows : (c + 1) * rows, :] = total

    return pl.pallas_call(
        body,
        out_shape=out,
        in_specs=[whole(x) for x in (info, *resid, *far, *returned)] + unread(after),
        out_specs=whole(out),
        scratch_shapes=[VMEM((half * cap, width), jnp.bfloat16)],
        compiler_params=params(24),
        cost_estimate=taking(microseconds),
        name="add_near",
    )(info, *resid, *far, *returned, *after)


def add_far(base, far):
    total, width = base.shape
    first = total - far.shape[0]
    out = jax.ShapeDtypeStruct(base.shape, jnp.bfloat16)

    def body(base_ref, far_ref, out_ref):
        if first:
            out_ref[:first, :] = base_ref[:first, :].astype(jnp.bfloat16)
        out_ref[first:, :] = (base_ref[first:, :] + far_ref[...].astype(jnp.float32)).astype(jnp.bfloat16)

    return pl.pallas_call(
        body,
        out_shape=out,
        in_specs=[whole(base), whole(far)],
        out_specs=whole(out),
        compiler_params=params(24),
        cost_estimate=taking(1),
        name="add_far",
    )(base, far)


def around(parts):
    moved = {d: exchange(parts[d], 2 * d) for d in reversed(range(1, len(parts)))}
    return [parts[0]] + [moved[d] for d in range(1, len(parts))]


def local(
    hidden_in,
    queries,
    token_keys,
    token_values,
    stored_keys,
    stored_values,
    cache_len,
    query_gain,
    k_gain,
    norm_gain,
    expert_ids,
    gate_weights,
    w_gate,
    w_up,
    w_down,
):
    token_rows, top = expert_ids.shape
    ep = lax.axis_size("ep")
    experts = ep // 2
    half = experts // 2
    slots = 2 * token_rows * top // experts
    chunks = 2 if slots >= 32 else 1
    cap = slots // chunks
    rows = token_rows // chunks
    arrays = (
        queries,
        hidden_in,
        stored_keys,
        stored_values,
        token_keys,
        token_values,
        query_gain,
        k_gain,
        norm_gain,
        expert_ids.T,
        gate_weights.T,
    )
    arrays = tuple(pltpu.with_memory_space_constraint(x, pltpu.HBM) for x in arrays)
    weights = (w_gate, w_up, w_down)
    weights = weights + tuple(exchange(w, 1) for w in weights)

    resid, normed, outgoing, info = [], [], [], None
    for c in range(chunks):
        residual, rows_c, outgoing, packed = attend(cache_len, arrays, normed, c, chunks, half, cap)
        info = packed if c == 0 else info
        resid.append(residual)
        normed.append(rows_c)
    far_rows = [exchange(normed[0], ep // 2)]
    gate = passed(outgoing, list(weights[3:]), 0.3)
    near = around(gate)
    after = gate[:1]
    for c in range(1, chunks):
        after = passed([normed[c]], after, 0.3)
        far_rows.append(exchange(after[0], ep // 2))

    placed = []
    for c in range(chunks):
        slotted, _ = relay(far_rows[c], top, half, cap, [], after, 0.5)
        placed.append(around(slotted))
        after = [slotted[0], *near]
    returned, after = [], after[:1]
    for c in range(chunks):
        outs = expert(placed[c], weights, half, after, 0.01)
        returned.append(around(outs))
        after = outs[:1]
    far_back, near_back = [], [None] * half
    for c in range(chunks):
        if c == chunks - 1:
            near_out = expert(near, weights, half, after, 4)
            near_back[0] = near_out[0]
            after = passed(near_out[half - 1 :], near_out[:1], 0.1)
            near_back[half - 1] = exchange(after[0], 2 * (half - 1))
        back = relay_back(returned[c], far_rows[c], top, cap, after, 0.6)
        far_back.append(exchange(back, ep // 2))
        after = [back]
    rest = passed(near_out[1 : half - 1], after, 0.1)
    for d in range(1, half - 1):
        near_back[d] = exchange(rest[d - 1], 2 * d)
    base = add_near(resid, far_back[:-1], near_back, info, cap, rest[:1], 4)
    return add_far(base, far_back[-1])


def solution(mesh):
    in_specs = (
        P(("grp", "ep"), None),
        P(("grp", "ep"), None),
        P(("grp", "ep"), None),
        P(("grp", "ep"), None),
        P(("grp", "ep"), None),
        P(("grp", "ep"), None),
        P(("grp", "ep")),
        P(),
        P(),
        P(),
        P(("grp", "ep"), None),
        P(("grp", "ep"), None),
        P(None, "ep"),
        P(None, "ep"),
        P("ep", None),
    )
    out_specs = P(("grp", "ep"), None)
    return jax.shard_map(local, mesh=mesh, in_specs=in_specs, out_specs=out_specs, check_vma=False)
```
